32 devices in a mesh: dom: 8 (over y, x, core), rep: 4 (over z).
Axes of the slice: x: 2, y: 2, z: 4, core: 2. Of those that a mesh axis runs over, the one named last changes fastest.
Arguments:
- codes: bfloat16 [16384, 256], P('dom'), may hold values from -1.5 to 1.5
- scales: bfloat16 [16384], P('dom'), may hold values from 0.5 to 2
- accum: float32 [16384], P('dom'), may hold values from 0.01 to 1
- relations: bfloat16 [64, 256], replicated, may hold values from -5 to 5
- matching: int32 [8], P('dom'), may hold values from 0 to 7, as said below
- edges: int32 [3, 131072], P(None, ('dom', 'rep')), may hold values from 0 to 2047, as said below
- counts: int32 [32], P(('dom', 'rep')), may hold values from 1 to 4096, 65536 in all
- negatives: int32 [256, 1024], P(('dom', 'rep')), may hold values from 0 to 2047
Outputs:
- new_codes: bfloat16 [16384, 256], P('dom')
- new_accum: float32 [16384], P(('dom', 'rep'))
The draws below stay inside these ranges and needn't reach their ends.
Inputs may be any that keep to these rules, and one draw needn't show every extreme that they name: matching[b] = b XOR m for one m from 1 to 7 shared by all buckets, so partitions pair up. `edges`: rows 0 and 2 hold row ids below 2048, row 1 relation ids below 64.
All inputs are finite; a program needn't handle non-finite values. No bound on the sum of `counts` on one device may be relied on, other than what follows from the above.
Results may differ from the reference program's by a relative error of at most 0.0075.
Values may be sent and summed in bfloat16 or wider, within the bound.
No kernel may reach another device: no remote copies, remote signals or barrier semaphores. Data moves between devices by JAX's collectives and lax.ppermute only.
A program may use at most 64 MiB of HBM per device.

```python
import math
import jax
import jax.numpy as jnp
import numpy as np
from jax import lax

D = 256
P_ROWS = 2048
GROUP = 512
NEG = 1024
CH_DEV = 8
REL = 64
PARTITIONS = 8
EDGE_SHARDS = 32
EDGES_DEV = 4096
EDGES = 131072
GROUPS = 256
ENTITIES = 16384
N_REP = 4


def draw_edges(key, part):
    key = jax.random.fold_in(key, 11)
    key_src, key_rel, key_dst = jax.random.split(key, 3)
    source = jax.random.randint(key_src, (EDGES,), 0, P_ROWS)
    relation = jax.random.randint(key_rel, (EDGES,), 0, REL)
    target = jax.random.randint(key_dst, (EDGES,), 0, P_ROWS)
    slot_pos = jnp.arange(EDGES)
    source = jnp.where(slot_pos == 0, P_ROWS - 1, source)
    target = jnp.where(slot_pos == 0, 0, target)
    return jnp.stack([source, relation, target]).astype(jnp.int32)


def draw_matching(key, part):
    key = jax.random.fold_in(key, 12)
    offset = jax.random.randint(key, (), 1, PARTITIONS)
    return jnp.bitwise_xor(jnp.arange(PARTITIONS, dtype=jnp.int32), offset.astype(jnp.int32))


def set_ends(drawn, stream_key, smallest, top_value):
    spot = [jax.random.randint(jax.random.fold_in(stream_key, axis), (), 0, length) for axis, length in enumerate(drawn.shape)]
    longest = drawn.shape.index(max(drawn.shape))
    neighbour = spot[:longest] + [(spot[longest] + 1) % drawn.shape[longest]] + spot[longest + 1:]
    return drawn.at[tuple(spot)].set(smallest).at[tuple(neighbour)].set(top_value)


def block_scale(own_key, extent, cuts, low, high):
    factor_of = 1.0
    for dim, parts in cuts:
        draws = jax.random.uniform(jax.random.fold_in(jax.random.fold_in(own_key, 6), dim), (parts,), jnp.float32, low / len(cuts), high / len(cuts))
        factor_of = factor_of * jnp.repeat(jnp.exp(draws), extent[dim] // parts).reshape((-1,) + (1,) * (len(extent) - 1 - dim))
    return factor_of


def split_up(count, total, most, skew):
    portions = [(1 << 20) // math.isqrt(grade ** skew) + 1 for grade in range(2, count + 1)]
    rest, holding = total - most - (count - 1), [1] * (count - 1)
    while rest > 0:
        free = [i for i in range(count - 1) if holding[i] < most]
        mass, budget = sum([portions[i] for i in free]), rest
        for i in free:
            more = min(most - holding[i], max(1, budget * portions[i] // mass), rest)
            holding[i] = holding[i] + more
            rest = rest - more
    return np.array([most] + holding)


def uneven(key, number_of, total, bound, slope):
    if number_of == 2:
        one = jax.random.randint(key, (), max(1, total - bound), min(bound, total - 1) + 1)
        return jnp.stack([one, total - one])
    sizes = jnp.asarray(split_up(number_of, total, bound, slope), jnp.int32)
    twos = (number_of - 1) // 2
    donor, sink = sizes[1:1 + 2 * twos:2], sizes[2:2 + 2 * twos:2]
    room = jnp.minimum(donor - 1, bound - sink)
    shifted = jax.random.randint(jax.random.fold_in(key, 1), (twos,), 0, 1 << 20) % (room + 1)
    sizes = sizes.at[1:1 + 2 * twos:2].set(donor - shifted).at[2:2 + 2 * twos:2].set(sink + shifted)
    return sizes[jax.random.permutation(jax.random.fold_in(key, 2), number_of)]


def bell_draw(rng, dims, scale, reach, pieces=(), held_as=jnp.bfloat16):
    loudness = block_scale(rng, dims, pieces, -0.22, 0.18) if pieces else 1.0
    entries = jax.random.normal(rng, dims, jnp.float32) * scale * loudness
    return jnp.minimum(jnp.maximum(entries, -reach), reach).astype(held_as)


def setup_inputs(seed: int = 0) -> dict:
    splits = jax.random.split(jax.random.key(seed), 9)
    codes = bell_draw(splits[0], (ENTITIES, D), 0.25, 1.5, ((0, 8),))
    scales = jnp.clip(jnp.exp(math.log(2.0) - 1.3862944 * jax.random.uniform(splits[1], (ENTITIES,), jnp.float32) ** block_scale(splits[1], (ENTITIES,), ((0, 8),), -0.2, 0.2)), 0.5, 2.0).astype(jnp.bfloat16)
    accum = jnp.clip(jnp.exp(math.log(1.0) - 4.6051702 * jax.random.uniform(splits[2], (ENTITIES,), jnp.float32) ** block_scale(splits[2], (ENTITIES,), ((0, 8),), -0.2, 0.2)), 0.01, 1.0)
    relations = bell_draw(splits[3], (REL, D), 1.0, 5.0)
    matching = draw_matching(jax.random.fold_in(splits[8], 71), 0)
    edges = draw_edges(jax.random.fold_in(splits[8], 71), 0)
    counts = uneven(splits[6], EDGE_SHARDS, EDGES_DEV * EDGE_SHARDS // 2, EDGES_DEV, 2).astype(jnp.int32)
    negatives = set_ends(jax.random.randint(splits[7], (GROUPS, NEG), 0, P_ROWS), jax.random.fold_in(splits[7], 1), 0, P_ROWS - 1).astype(jnp.int32)
    return {"codes": codes, "scales": scales, "accum": accum, "relations": relations, "matching": matching, "edges": edges, "counts": counts, "negatives": negatives}


LEARN_RATE = 0.1
ROOT_EPSILON = 1e-08

def group_terms(src_block, dst_block, relation_rows, src_ids, dst_ids, live_mask, negative_ids):
    source_rows = jnp.take(src_block, src_ids, axis=0).astype(jnp.float32)
    target_rows = jnp.take(dst_block, dst_ids, axis=0)
    negative_rows = jnp.take(dst_block, negative_ids, axis=0)
    relation_f = relation_rows.astype(jnp.float32)
    query = (source_rows * relation_f).astype(jnp.bfloat16)
    positive = lax.optimization_barrier(jnp.sum(query.astype(jnp.float32) * target_rows.astype(jnp.float32), axis=1))
    scores = jnp.dot(query, negative_rows.T, preferred_element_type=jnp.float32)
    weight = live_mask.astype(jnp.float32)
    pos_coef = -weight * jax.nn.sigmoid(-positive)
    neg_coef = (weight[:, None] * jax.nn.sigmoid(scores) / negative_rows.shape[0]).astype(jnp.bfloat16)
    query_grad = pos_coef[:, None] * target_rows.astype(jnp.float32) + jnp.dot(neg_coef, negative_rows, preferred_element_type=jnp.float32)
    source_grad = query_grad * relation_f
    target_grad = pos_coef[:, None] * query.astype(jnp.float32)
    negative_grad = jnp.dot(neg_coef.T, query, preferred_element_type=jnp.float32)
    return (source_grad, target_grad, negative_grad)

def reference(codes, scales, accum, relations, matching, edges, counts, negatives):
    values = codes.astype(jnp.float32) * scales.astype(jnp.float32)[:, None]
    rounded = values.astype(jnp.bfloat16).reshape(PARTITIONS, P_ROWS, D)
    per_bucket = N_REP * CH_DEV
    edge_ids = edges.reshape(3, PARTITIONS, per_bucket, GROUP)
    slot_pos = jnp.arange(EDGES_DEV, dtype=jnp.int32)
    live_all = (slot_pos[None, :] < counts[:, None]).astype(jnp.int32).reshape(PARTITIONS, per_bucket, GROUP)
    neg_all = negatives.reshape(PARTITIONS, per_bucket, NEG)

    def bucket(gradients, owner):
        partner = matching[owner]
        src_block = rounded[owner]
        dst_block = rounded[partner]

        def group_step(carry, group_at):
            src_ids = edge_ids[0, owner, group_at]
            rel_ids = edge_ids[1, owner, group_at]
            dst_ids = edge_ids[2, owner, group_at]
            live_mask = live_all[owner, group_at]
            negative_ids = neg_all[owner, group_at]

            def score_group(grads_in):
                relation_rows = jnp.take(relations, rel_ids, axis=0)
                source_grad, target_grad, negative_grad = group_terms(src_block, dst_block, relation_rows, src_ids, dst_ids, live_mask, negative_ids)
                first = grads_in[0].at[src_ids].add(source_grad)
                second = grads_in[1].at[dst_ids].add(target_grad).at[negative_ids].add(negative_grad)
                return (first, second)
            result = lax.cond(jnp.any(live_mask > 0), score_group, lambda grads_in: grads_in, carry)
            return (result, None)
        empty = jnp.zeros((P_ROWS, D), jnp.float32)
        (src_total, dst_total), _ = lax.scan(group_step, (empty, empty), jnp.arange(per_bucket, dtype=jnp.int32))
        gradients = gradients.at[owner].add(src_total).at[partner].add(dst_total)
        return (gradients, None)
    start_grads = jnp.zeros((PARTITIONS, P_ROWS, D), jnp.float32)
    grad_all, _ = lax.scan(bucket, start_grads, jnp.arange(PARTITIONS, dtype=jnp.int32))
    grad_all = grad_all.reshape(ENTITIES, D)
    new_accum = accum + lax.optimization_barrier(jnp.mean(grad_all * grad_all, axis=1))
    updated = values - LEARN_RATE * grad_all / (jnp.sqrt(new_accum)[:, None] + ROOT_EPSILON)
    new_codes = (updated / scales.astype(jnp.float32)[:, None]).astype(jnp.bfloat16)
    return (new_codes, new_accum)
```

```python
import functools

import jax
import jax.numpy as jnp
from jax import lax
from jax.experimental import pallas as pl
from jax.experimental.pallas import tpu as pltpu
from jax.sharding import PartitionSpec as P

GROUP = 512
LOW = 128
TILE = 512
NARROW = 256
HELD = 10
LAST_KEY = 2**31 - 1
LEARN_RATE = 0.1
ROOT_EPSILON = 1e-08
VMEM_LIMIT = 24 * 1024 * 1024


def swap_beside(apart, block, beside, *args):
    count = lax.axis_size("dom")

    def route(bits):
        return [(at, at ^ bits) for at in range(count)]

    if count <= 8:

        def branch(bits):
            return lambda block, *args: (lax.ppermute(block, "dom", route(bits)),) + beside(*args)

        return lax.switch(apart - 1, [branch(bits) for bits in range(1, count)], block, *args)
    for bit in range(count.bit_length() - 1):
        here = jnp.bitwise_and(jnp.right_shift(apart, bit), 1) == 1
        block = lax.cond(here, lambda b: lax.ppermute(b, "dom", route(1 << bit)), lambda b: b, block)
    return (block,) + beside(*args)


def ring_order(count):
    return list(range(0, count, 2)) + list(range(1, count, 2))[::-1]


def one_hot(rows, ids, one=1):
    step = min(rows, 256)
    spots = lax.broadcasted_iota(jnp.int32, (step, ids.shape[1]), 0).astype(jnp.bfloat16)
    low = (ids & (step - 1)).astype(jnp.float32)
    parts = []
    for first in range(0, rows, step):
        inside = (ids >= first) & (ids < first + step)
        key = jnp.where(inside, low, -1.0).astype(jnp.bfloat16)
        parts.append(jnp.where(spots == key, jnp.bfloat16(one), jnp.bfloat16(0)))
    return jnp.concatenate(parts, axis=0) if len(parts) > 1 else parts[0]


def nt_dot(a, b):
    return lax.dot_general(a, b, (((1,), (1,)), ((), ())), preferred_element_type=jnp.float32)


def nn_dot(a, b):
    return jnp.dot(a, b, preferred_element_type=jnp.float32)


def unpack(words):
    return jnp.concatenate([words & 0xFFFF, words >> 16], axis=0)


def bits_for(count):
    return (count - 1).bit_length()


class Packing:
    def __init__(self, part_rows, share, relations, blocks):
        self.half = part_rows // 2
        self.relation_at = bits_for(blocks)
        self.target_at = self.relation_at + bits_for(relations)
        self.source_at = self.target_at + bits_for(share + 1)
        assert self.source_at + bits_for(part_rows) <= 32

    def pack(self, source, target, relation, block):
        return (
            ((source - self.half) << self.source_at)
            + (target << self.target_at)
            + (relation << self.relation_at)
            + block
        )

    def bound(self, row):
        return (row - self.half) << self.source_at

    def source(self, word):
        return (word >> self.source_at) + self.half

    def target(self, word):
        return (word >> self.target_at) & ((1 << (self.source_at - self.target_at)) - 1)

    def relation(self, word):
        return (word >> self.relation_at) & ((1 << (self.target_at - self.relation_at)) - 1)

    def is_empty(self, word):
        return self.target(word) == (1 << (self.source_at - self.target_at)) - 1

    def block(self, word):
        return word & ((1 << self.relation_at) - 1)


def sort_columns(parts):
    count = len(parts)
    list_bits = bits_for(count)
    column = count * 8
    spread = max(1, TILE // column)
    low_lane_bits = bits_for(spread)
    lane_bits = [7 - low_lane_bits + k for k in range(low_lane_bits)] + list(range(7 - low_lane_bits))
    places = [("list", k) for k in range(list_bits)] + [("row", k) for k in range(3)] + [("lane", k) for k in lane_bits]
    row = lax.broadcasted_iota(jnp.int32, (8, 128), 0)
    lane = lax.broadcasted_iota(jnp.int32, (8, 128), 1)
    unset = {
        place: ((row if place[0] == "row" else lane) & (1 << place[1])) == 0
        for place in places
        if place[0] != "list"
    }
    total = len(places)

    def is_unset(index, position):
        if position == total:
            return True
        kind, bit = places[position]
        return index & (1 << bit) == 0 if kind == "list" else unset[(kind, bit)]

    def choose(mask, yes, no):
        if mask is True or mask is False:
            return yes if mask else no
        return jnp.where(mask, yes, no)

    for size in range(1, total + 1):
        for position in range(size - 1, -1, -1):
            kind, bit = places[position]
            if kind == "list":
                done = list(parts)
                for low in range(count):
                    high = low | 1 << bit
                    if high == low:
                        continue
                    up = is_unset(low, size)
                    small, large = jnp.minimum(parts[low], parts[high]), jnp.maximum(parts[low], parts[high])
                    done[low], done[high] = choose(up, small, large), choose(up, large, small)
                parts = done
                continue
            axis, extent = (0, 8) if kind == "row" else (1, 128)
            apart = 1 << bit
            first = unset[(kind, bit)]
            done = []
            for index, part in enumerate(parts):
                other = pltpu.roll(part, apart, axis)
                if 2 * apart != extent:
                    other = jnp.where(first, pltpu.roll(part, extent - apart, axis), other)
                small, large = jnp.minimum(part, other), jnp.maximum(part, other)
                up = is_unset(index, size)
                if up is True:
                    keep_small = first
                elif up is False:
                    keep_small = jnp.logical_not(first)
                else:
                    keep_small = jnp.logical_not(jnp.logical_xor(first, up))
                done.append(jnp.where(keep_small, small, large))
            parts = done
    return parts


def pick(table, place):
    out = jnp.int32(table[0])
    for at, entry in enumerate(table[1:], 1):
        out = jnp.where(place == at, jnp.int32(entry), out)
    return out


def open_kernel(tiles, share, place_ref, codes_hbm, scales_hbm, relations_hbm, edges_hbm, negatives_hbm, counts_hbm, *refs):
    reps = len(refs) - 11
    outs, refs = refs[:reps], refs[reps:]
    own_t_ref, values_t_ref, rel_t_ref, codes_ref, scales_ref, relations_ref, edges_ref, negatives_ref, counts_ref, counted, sems = refs
    place = place_ref[0]
    first = pl.multiple_of(place * share, 128)
    pairs = [
        (negatives_hbm, negatives_ref),
        (counts_hbm, counts_ref),
        (edges_hbm, edges_ref),
        (codes_hbm.at[pl.ds(first, share), :], codes_ref),
        (scales_hbm, scales_ref),
        (relations_hbm, relations_ref),
    ]
    copies = [pltpu.make_async_copy(source, target, sems.at[k]) for k, (source, target) in enumerate(pairs)]
    for copy in copies:
        copy.start()
    lanes = counted.shape[0]
    copies[0].wait()
    for block in range(tiles):
        negative = negatives_ref[block : block + 1, :]
        near = one_hot(LOW, negative & (LOW - 1))
        far = one_hot(lanes, negative >> (LOW.bit_length() - 1))
        held = nt_dot(far, near)
        for k in range(lanes):
            counted[k, block : block + 1, :] = held[k : k + 1, :]
    copies[1].wait()
    copies[2].wait()
    for apart, ids_ref in enumerate(outs):
        for tile in range(tiles):
            span = slice(tile * GROUP, (tile + 1) * GROUP)
            ids_ref[tile : tile + 1, :] = edges_ref[0:1, span] | (edges_ref[2:3, span] << 16)
        for tile in range(tiles // 2):
            near = edges_ref[1:2, tile * GROUP : (tile + 1) * GROUP]
            far = edges_ref[1:2, (tiles // 2 + tile) * GROUP : (tiles // 2 + tile + 1) * GROUP]
            ids_ref[tiles + tile : tiles + tile + 1, :] = near | (far << 16)
        to = place + apart
        to = jnp.where(to >= reps, to - reps, to)
        held = [counted[to * (share // LOW) + k] for k in range(share // LOW)]
        held += [jnp.zeros((tiles, GROUP - share), jnp.float32)] * (share < GROUP)
        held = jnp.concatenate(held, axis=1).astype(jnp.int32)
        ids_ref[3 * tiles // 2 : 2 * tiles, :] = held[: tiles // 2] | (held[tiles // 2 :] << 16)
        ids_ref[2 * tiles : 2 * tiles + 1, :] = jnp.full((1, GROUP), counts_ref[0], jnp.int32)
    for copy in copies[3:]:
        copy.wait()
    values_t = codes_ref[...].T.astype(jnp.float32) * scales_ref[:, pl.ds(first, share)].astype(jnp.float32)
    values_t_ref[...] = values_t
    own_t_ref[...] = values_t.astype(jnp.bfloat16)
    rel_t_ref[...] = relations_ref[...].T


def source_kernel(codes_ref, scales_ref, src_t_ref):
    codes_t = codes_ref[...].T.astype(jnp.float32)
    src_t_ref[...] = (codes_t * scales_ref[...].astype(jnp.float32)).astype(jnp.bfloat16)


def sort_kernel(packing, tiles, share, place_ref, *refs):
    ids_refs, (keys_ref, below_ref, ends_ref, ends_held, sem) = refs[:-5], refs[-5:]
    shards = len(ids_refs)
    first = place_ref[0] * share
    row = lax.broadcasted_iota(jnp.int32, (8, 128), 0)
    lane = lax.broadcasted_iota(jnp.int32, (8, 128), 1)
    keys, ranks, dead = [], [], jnp.zeros((1, 128), jnp.int32)
    for shard, ids_ref in enumerate(ids_refs):
        live = ids_ref[2 * tiles : 2 * tiles + 1, 0:128]
        relations = unpack(ids_ref[tiles : 3 * tiles // 2, :])
        for top in range(0, tiles, 8):
            for left in range(0, GROUP, 128):
                word = ids_ref[top : top + 8, left : left + 128]
                relation = relations[top : top + 8, left : left + 128]
                target = (word >> 16) - first
                target = jnp.where((target >= 0) & (target < share), target, share)
                key = packing.pack(word & 0xFFFF, target, relation, shard * tiles + top + row)
                over = (top + row) * GROUP + left + lane - live
                keys.append(jnp.where(over < 0, key, LAST_KEY))
                ranks.append(jnp.where(over < 0, LAST_KEY, over + dead))
        dead = dead + (tiles * GROUP - live)
    below = [jnp.int32(0)]
    for at in range(1, shards + 1):
        bound = LAST_KEY if at == shards else packing.bound(at * share)
        inside = functools.reduce(jnp.add, [jnp.where(key < bound, 1.0, 0.0) for key in keys])
        below.append(jnp.sum(inside).astype(jnp.int32))
    fill = [(below[at] - below[at + 1]) & (TILE - 1) for at in range(shards)]
    enough = functools.reduce(jnp.add, fill) <= len(keys) * 1024 - below[-1]
    filled = [jnp.int32(0)]
    for at in range(shards):
        filled.append(filled[at] + jnp.where(enough, fill[at], 0))
    for at in range(shards + 1):
        below_ref[at] = below[at] + filled[at]
    parts = []
    for key, rank in zip(keys, ranks):
        for at in range(shards - 2, -1, -1):
            key = jnp.where(rank < filled[at + 1], packing.bound((at + 1) * share) - 1, key)
        parts.append(key)
    parts = sort_columns(parts)
    ends_held[...] = jnp.zeros_like(ends_held)
    ends_held[0:1, :] = parts[0][0:1, :]
    ends_held[1:2, :] = parts[-1][7:8, :]
    copy = pltpu.make_async_copy(ends_held, ends_ref, sem)
    copy.start()
    columns = jnp.concatenate(parts, axis=0).T
    spread = max(1, TILE // columns.shape[1])
    rows = columns.shape[0] // spread
    for k in range(spread):
        keys_ref[:rows, k * columns.shape[1] : (k + 1) * columns.shape[1]] = columns[k * rows : (k + 1) * rows]
    keys_ref[rows:, :] = jnp.full((keys_ref.shape[0] - rows, TILE), LAST_KEY, jnp.int32)
    copy.wait()


def part_kernel(packing, tables, opening, closing, negs, place_ref, below_ref, ends_ref, keys_ref, src_t_ref, rel_t_ref, dst_t_ref, *refs):
    refs = list(refs)
    src_total = refs.pop()
    if closing:
        *refs, coef_ref, query_ref, relation_ref, new_query_ref, new_relation_ref, dst_total = refs
        half_ref, times_ref, before_ref, *given, after_ref, src_grad_ref, dst_grad_ref, coefs_ref = refs
        dst_total[...] = before_ref[...]
        for held, source in zip((coef_ref, query_ref, relation_ref, new_query_ref, new_relation_ref), given):
            held[...] = source[...]
    elif opening:
        *ids_refs, src_grad_ref, dst_total, coef_ref, query_ref, relation_ref, new_query_ref, new_relation_ref, half_ref, times_ref = refs
        half_ref[...] = dst_t_ref[...].T * jnp.bfloat16(0.5)
        tiles = ids_refs[0].shape[0] // 2
        counted = [unpack(ids_ref[3 * tiles // 2 : 2 * tiles, : half_ref.shape[0]]) for ids_ref in ids_refs]
        counted = jnp.concatenate(counted, axis=0).astype(jnp.float32) * (0.5 / negs)
        times_ref[...] = counted.T.astype(times_ref.dtype)
        dst_total[...] = jnp.zeros_like(dst_total)
    else:
        half_ref, times_ref = refs[:2]
        src_grad_ref, dst_total, coef_ref, query_ref, relation_ref, new_query_ref, new_relation_ref = refs[-7:]
    share, width = half_ref.shape

    def span(table):
        at = pick(table, place_ref[0])
        start = pl.multiple_of(at * share, 128)
        begin = below_ref[at] // TILE
        return start, begin, jnp.maximum((below_ref[at + 1] + TILE - 1) // TILE, begin + 1)

    spans = [span(table) for table in tables]
    spans = spans + spans[-1:] * (3 - len(spans))
    start, begin, end = spans[0]
    src_total[...] = jnp.zeros_like(src_total)
    last_row = keys_ref.shape[0] - 9

    def after(at):
        (_, _, end0), (start1, begin1, end1), (start2, begin2, _) = spans
        over, soon, over1 = at + 1 >= end0, at + 2 >= end0, begin1 + 1 >= end1
        one = jnp.where(over, begin1, at + 1)
        two = jnp.where(over, jnp.where(over1, begin2, begin1 + 1), jnp.where(soon, begin1, at + 2))
        two_start = jnp.where(over, jnp.where(over1, start2, start1), jnp.where(soon, start1, start))
        return one, two, pl.multiple_of(two_start, 128)

    def word_of(at):
        return keys_ref[pl.ds(at, 1), :]

    def window(at, start):
        at = jnp.minimum(at, last_row)
        low = packing.source(ends_ref[0, at]) - start
        high = packing.source(ends_ref[1, at + 127 - last_row]) - start
        low = jnp.clip((low >> 7) << 7, 0, share - NARROW)
        return pl.multiple_of(low, 128), jnp.minimum(high, share - 1) - low < NARROW

    def sources(word, start, extent):
        return one_hot(extent, jnp.where(packing.is_empty(word), -1, packing.source(word) - start))

    def query_of(word, start, extent):
        relation = nn_dot(rel_t_ref[...], one_hot(rel_t_ref.shape[1], packing.relation(word)))
        relation = relation.astype(jnp.bfloat16)
        found = nn_dot(src_t_ref[:, pl.ds(start, extent)], sources(word, start, extent))
        return found.astype(jnp.bfloat16) * relation, relation

    def coef_of(word, query):
        times = nn_dot(times_ref[...], one_hot(times_ref.shape[1], packing.block(word)))
        bend = jnp.tanh(nn_dot(half_ref[...], query))
        below = (bend - 1.0).astype(jnp.bfloat16)
        return (times * (bend + 1.0)).astype(jnp.bfloat16) + one_hot(share, packing.target(word), 0.5) * below

    def keep(coef, query, relation, new_query, new_relation):
        coef_ref[...] = coef
        query_ref[...] = query
        relation_ref[...] = relation
        new_query_ref[...] = new_query
        new_relation_ref[...] = new_relation

    if opening:
        query, relation = query_of(word_of(begin), start, share)
        one, _, _ = after(begin)
        one_start = pl.multiple_of(jnp.where(begin + 1 >= end, spans[1][0], start), 128)
        new_query, new_relation = query_of(word_of(one), one_start, share)
        keep(coef_of(word_of(begin), query), query, relation, new_query, new_relation)

    def work(at, one, two, low, two_from, extent):
        coef, query, relation = coef_ref[...], query_ref[...], relation_ref[...]
        new_query, new_relation = new_query_ref[...], new_relation_ref[...]
        back = nn_dot(dst_t_ref[...], coef)
        third_query, third_relation = query_of(word_of(two), two_from, extent)
        new_coef = coef_of(word_of(one), new_query)
        dst_total[...] += nt_dot(coef, query)
        back = back.astype(jnp.bfloat16) * relation
        src_total[pl.ds(low, extent), :] += nt_dot(sources(word_of(at), start + low, extent), back)
        keep(new_coef, new_query, new_relation, third_query, third_relation)

    def light_work(at, one, two, low, two_from, extent):
        coef, query = coef_ref[...], query_ref[...]
        new_query, new_relation = new_query_ref[...], new_relation_ref[...]
        third_query, third_relation = query_of(word_of(two), two_from, extent)
        new_coef = coef_of(word_of(one), new_query)
        dst_total[...] += nt_dot(coef, query)
        coefs_ref[at - begin] = coef
        keep(new_coef, new_query, new_relation, third_query, third_relation)

    def step_with(work):
        def step(at, carry):
            one, two, two_start = after(at)
            if share <= NARROW:
                work(at, one, two, 0, two_start, share)
                return carry
            low, fits = window(at, start)
            two_low, two_fits = window(two, two_start)
            narrow = jnp.logical_and(fits, two_fits)

            @pl.when(narrow)
            def _():
                work(at, one, two, low, pl.multiple_of(two_start + two_low, 128), NARROW)

            @pl.when(jnp.logical_not(narrow))
            def _():
                work(at, one, two, 0, two_start, share)

            return carry

        return step

    light = begin
    if closing:
        light = jnp.minimum(end, begin + HELD)
        lax.fori_loop(begin, light, step_with(light_work), 0)
    lax.fori_loop(light, end, step_with(work), 0)
    src_grad_ref[...] = src_total[...].astype(src_grad_ref.dtype)
    if closing:
        dst_grad_ref[...] = dst_total[...].astype(dst_grad_ref.dtype)


def finish_kernel(packing, owners, place_ref, below_ref, keys_ref, src_grad_ref, rel_t_ref, dst_t_ref, coefs_ref, own_ref, src_total):
    share = own_ref.shape[0]
    at = pick(owners, place_ref[0])
    start = at * share
    begin = below_ref[at] // TILE
    end = jnp.maximum((below_ref[at + 1] + TILE - 1) // TILE, begin + 1)
    src_total[...] = src_grad_ref[...]

    def step(at, carry):
        word = keys_ref[pl.ds(at, 1), :]
        relation = nn_dot(rel_t_ref[...], one_hot(rel_t_ref.shape[1], packing.relation(word)))
        back = (nn_dot(dst_t_ref[...], coefs_ref[at - begin]) * relation).astype(jnp.bfloat16)
        source = one_hot(share, jnp.where(packing.is_empty(word), -1, packing.source(word) - start))
        src_total[...] += nt_dot(source, back)
        return carry

    lax.fori_loop(begin, jnp.minimum(end, begin + HELD), step, 0)
    own_ref[...] = src_total[...].astype(own_ref.dtype)


def update_kernel(place_ref, values_t_ref, scales_ref, accum_ref, arrived_ref, own_ref, returned_ref, piece_ref, low_ref, high_ref, state_ref):
    share = arrived_ref.shape[0]
    first = pl.multiple_of(place_ref[0] * share, 128)
    summed = arrived_ref[...].astype(jnp.float32) + own_ref[...].astype(jnp.float32)
    summed = (summed + returned_ref[...].astype(jnp.float32)).T
    scale = scales_ref[:, pl.ds(first, share)].astype(jnp.float32)
    state = accum_ref[:, pl.ds(first, share)] + jnp.mean(summed * summed, axis=0, keepdims=True)
    updated = values_t_ref[...] - summed * (LEARN_RATE / (jnp.sqrt(state) + ROOT_EPSILON))
    piece = (updated * (1.0 / scale)).T.astype(piece_ref.dtype)
    piece_ref[...] = piece
    low_ref[...] = piece[: share // 2]
    high_ref[...] = piece[share // 2 :]
    state_ref[...] = state


def place_kernel(tables, unit, place_ref, *refs):
    pieces, (out_ref, sems) = refs[: len(tables)], refs[-2:]
    place = place_ref[0]
    for k, (table, chosen) in enumerate(tables):
        row = pl.multiple_of(pick(table, place) * unit, 128)
        copy = pltpu.make_async_copy(pieces[k], out_ref.at[pl.ds(row, pieces[k].shape[0]), :], sems.at[k])
        if chosen is None:
            copy.start()
            continue

        @pl.when(pick(chosen, place) == 1)
        def _(copy=copy):
            copy.start()
            copy.wait()

    for k, (table, chosen) in enumerate(tables):
        if chosen is None:
            row = pl.multiple_of(pick(table, place) * unit, 128)
            pltpu.make_async_copy(pieces[k], out_ref.at[pl.ds(row, pieces[k].shape[0]), :], sems.at[k]).wait()


SMEM = pl.BlockSpec(memory_space=pltpu.SMEM)
VMEM = pl.BlockSpec(memory_space=pltpu.VMEM)


ANY = pl.BlockSpec(memory_space=pl.ANY)
HBM = pl.BlockSpec(memory_space=pltpu.HBM)


def call(kernel, inputs, outs, scratch, name, us, scalars=1, unread=0, aliases={}, scalar_outs=(), in_hbm=0, out=None, grant=VMEM_LIMIT):
    return pl.pallas_call(
        kernel,
        out_shape=outs,
        in_specs=[SMEM] * scalars + [HBM] * in_hbm + [VMEM] * (len(inputs) - scalars - in_hbm - unread) + [ANY] * unread,
        out_specs=out or ([SMEM if at in scalar_outs else VMEM for at in range(len(outs))] if isinstance(outs, tuple) else VMEM),
        scratch_shapes=scratch,
        input_output_aliases=aliases,
        compiler_params=pltpu.CompilerParams(vmem_limit_bytes=grant),
        cost_estimate=pl.CostEstimate(flops=int(us * 1.15e9), bytes_accessed=0, transcendentals=0),
        name=name,
    )(*inputs)


def body(codes, scales, accum, relations, matching, edges, counts, negatives):
    reps = lax.axis_size("rep")
    at_rep = lax.axis_index("rep")
    place = at_rep[None]
    apart_dom = jnp.bitwise_xor(matching[0], lax.axis_index("dom"))
    part_rows, width = codes.shape
    slots = edges.shape[1]
    tiles = slots // GROUP
    negs = negatives.shape[1]
    share = part_rows // reps
    scales_row, accum_row = scales[None], accum[None]

    shape = jax.ShapeDtypeStruct
    ids_shape = shape((2 * tiles + 1, GROUP), jnp.int32)
    *sent, own_t, values_t, rel_t = call(
        functools.partial(open_kernel, tiles, share),
        (place, codes, scales_row, relations, edges, negatives, counts),
        (ids_shape,) * reps
        + (shape((width, share), jnp.bfloat16), shape((width, share), jnp.float32),
           shape(relations.shape[::-1], jnp.bfloat16)),
        [pltpu.VMEM((share, width), codes.dtype), pltpu.VMEM(scales_row.shape, scales.dtype),
         pltpu.VMEM(relations.shape, relations.dtype), pltpu.VMEM(edges.shape, edges.dtype),
         pltpu.VMEM(negatives.shape, negatives.dtype), pltpu.SMEM(counts.shape, counts.dtype),
         pltpu.VMEM((part_rows // LOW, tiles, LOW), jnp.float32), pltpu.SemaphoreType.DMA((6,))],
        "open", 3, in_hbm=6, grant=56 * 1024 * 1024)

    part = shape((share, width), jnp.bfloat16)
    part_sum = shape((share, width), jnp.float32)
    total = pltpu.VMEM((share, width), jnp.float32)
    packing = Packing(part_rows, share, relations.shape[0], reps * tiles)

    @jax.jit
    def sort_edges(place, *ids):
        return call(
            functools.partial(sort_kernel, packing, tiles, share), (place, *ids),
            (shape((reps * slots // TILE + 8, TILE), jnp.int32), shape((reps + 1,), jnp.int32),
             shape((8, 128), jnp.int32)),
            [pltpu.VMEM((8, 128), jnp.int32), pltpu.SemaphoreType.DMA], "sort", 5, scalar_outs=(1, 2),
            grant=40 * 1024 * 1024)

    def gather_edges(place, codes, scales_row, *sent):
        ids = [sent[0]]
        for apart in range(1, reps):
            along = [(at, (at + apart) % reps) for at in range(reps)]
            ids.append(lax.ppermute(sent[apart], "rep", along))
        src_t = call(source_kernel, (codes, scales_row), shape((width, part_rows), jnp.bfloat16), [], "source", 2, scalars=0)
        return (src_t, *ids) + tuple(sort_edges(place, *ids))

    dst_t, src_t, *ids, keys, below, ends = swap_beside(
        apart_dom, own_t, gather_edges, place, codes, scales_row, *sent)

    order = ring_order(reps)
    forward = [(order[i], order[(i + 1) % reps]) for i in range(reps)]

    def owners(behind):
        return [order[(order.index(z) - behind) % reps] for z in range(reps)]

    wide = shape((share, TILE), jnp.bfloat16)
    tall = shape((width, TILE), jnp.bfloat16)
    state = [wide, tall, tall, tall, tall]
    moving = arrived = None
    for behind in range(1, reps + 1):
        opening, closing = behind == 1, behind == reps
        table = owners(behind)
        chain = [owners(later) for later in range(behind, min(behind + 2, reps) + 1)]
        kept = shape((HELD, share, TILE), jnp.bfloat16)
        outs = (part_sum, part, kept) if closing else (part, part_sum, *state)
        scratch = ([pltpu.VMEM(kept.shape, kept.dtype) for kept in state] + [total] if closing else []) + [total]
        if opening:
            given = tuple(ids)
            outs += (part, shape((share, reps * tiles), jnp.bfloat16))
        else:
            given = (half, times, dst_grad) + held + (arrived if arrived is not None else below,)
        done = call(
            functools.partial(part_kernel, packing, chain, opening, closing, negs),
            (place, below, ends, keys, src_t, rel_t, dst_t) + given, outs, scratch, "part", 9,
            scalars=3, unread=0 if opening else 1,
            aliases={} if opening or closing else {9 + k: 1 + k for k in range(6)})
        src_grad, dst_grad = done[:2]
        held = tuple(done[2:7])
        if opening:
            half, times = done[7:]
            moving = src_grad
        elif not closing:
            arrived = lax.ppermute(moving, "rep", forward)
            moving = (arrived.astype(jnp.float32) + src_grad.astype(jnp.float32)).astype(jnp.bfloat16)
    arrived = lax.ppermute(moving, "rep", forward)
    @jax.jit
    def finish(*given):
        return call(functools.partial(finish_kernel, packing, table), given, part, [total], "finish", 3, scalars=2)

    returned, own = swap_beside(
        apart_dom, dst_grad, lambda *given: (finish(*given),), place, below, keys, src_grad, rel_t, dst_t, done[2])

    half_part = shape((share // 2, width), jnp.bfloat16)
    piece, low, high, state = call(
        update_kernel, (place, values_t, scales_row, accum_row, arrived, own, returned),
        (part, half_part, half_part, shape((1, share), jnp.float32)), [], "update", 2)

    def put(tables, pieces, given, us):
        return call(
            functools.partial(place_kernel, tables, share // 2), (place, *pieces) + given, shape(codes.shape, jnp.bfloat16),
            [pltpu.SemaphoreType.DMA((len(pieces),))], "place", us, unread=len(given),
            aliases={1 + len(pieces): 0} if given else {}, out=HBM)

    if reps == 4:
        across = [(0, 2), (2, 0), (1, 3), (3, 1)]
        far = [lax.ppermute(held, "rep", across) for held in (low, high)]
        near = lax.ppermute(piece, "rep", [(0, 1), (1, 0), (2, 3), (3, 2)])
        middle = lax.ppermute(piece, "rep", [(1, 2), (2, 1)])
        ends = [lax.ppermute(held, "rep", [(2, 3), (1, 0)]) for held in far]
        early = [(piece, ([0, 2, 4, 6], None)), (near, ([2, 0, 6, 4], None))]
        early += [(held, ([4 + k, 6 + k, k, 2 + k], None)) for k, held in enumerate(far)]
        late = [(middle, ([6, 4, 2, 0], [0, 1, 1, 0]))]
        late += [(held, ([6 + k, 4 + k, 2 + k, k], [1, 0, 0, 1])) for k, held in enumerate(ends)]
    else:
        pieces = [piece]
        for behind in range(1, reps):
            pieces.append(lax.ppermute(pieces[-1], "rep", forward))
        early = [(held, ([2 * at for at in owners(behind)], None)) for behind, held in enumerate(pieces)]
        early, late = early[:-1], early[-1:]
    new_codes = put([table for _, table in early], [held for held, _ in early], (), 1)
    new_codes = put([table for _, table in late], [held for held, _ in late], (new_codes,), 1)
    return (new_codes, state[0])


def solution(mesh):
    placed = (
        P("dom", None),
        P("dom"),
        P("dom"),
        P(),
        P("dom"),
        P(None, ("dom", "rep")),
        P(("dom", "rep")),
        P(("dom", "rep"), None),
    )
    return jax.shard_map(
        body,
        mesh=mesh,
        in_specs=placed,
        out_specs=(P("dom", None), P(("dom", "rep"))),
        check_vma=False,
    )
```

```python
import functools

import jax
import jax.numpy as jnp
from jax import lax
from jax.experimental import pallas as pl
from jax.experimental.pallas import tpu as pltpu
from jax.sharding import PartitionSpec as P

GROUP = 512
LOW = 128
TILE = 512
NARROW = 256
HELD = 10
LAST_KEY = 2**31 - 1
LEARN_RATE = 0.1
ROOT_EPSILON = 1e-08
VMEM_LIMIT = 24 * 1024 * 1024


def swap_beside(apart, block, beside, *args):
    count = lax.axis_size("dom")

    def route(bits):
        return [(at, at ^ bits) for at in range(count)]

    if count <= 8:

        def branch(bits):
            return lambda block, *args: (lax.ppermute(block, "dom", route(bits)),) + beside(*args)

        return lax.switch(apart - 1, [branch(bits) for bits in range(1, count)], block, *args)
    for bit in range(count.bit_length() - 1):
        here = jnp.bitwise_and(jnp.right_shift(apart, bit), 1) == 1
        block = lax.cond(here, lambda b: lax.ppermute(b, "dom", route(1 << bit)), lambda b: b, block)
    return (block,) + beside(*args)


def ring_order(count):
    return list(range(0, count, 2)) + list(range(1, count, 2))[::-1]


def one_hot(rows, ids, one=1):
    step = min(rows, 256)
    spots = lax.broadcasted_iota(jnp.int32, (step, ids.shape[1]), 0).astype(jnp.bfloat16)
    low = (ids & (step - 1)).astype(jnp.float32)
    parts = []
    for first in range(0, rows, step):
        inside = (ids >= first) & (ids < first + step)
        key = jnp.where(inside, low, -1.0).astype(jnp.bfloat16)
        parts.append(jnp.where(spots == key, jnp.bfloat16(one), jnp.bfloat16(0)))
    return jnp.concatenate(parts, axis=0) if len(parts) > 1 else parts[0]


def nt_dot(a, b):
    return lax.dot_general(a, b, (((1,), (1,)), ((), ())), preferred_element_type=jnp.float32)


def nn_dot(a, b):
    return jnp.dot(a, b, preferred_element_type=jnp.float32)


def unpack(words):
    return jnp.concatenate([words & 0xFFFF, words >> 16], axis=0)


def bits_for(count):
    return (count - 1).bit_length()


class Packing:
    def __init__(self, part_rows, share, relations, blocks):
        self.half = part_rows // 2
        self.relation_at = bits_for(blocks)
        self.target_at = self.relation_at + bits_for(relations)
        self.source_at = self.target_at + bits_for(share + 1)
        assert self.source_at + bits_for(part_rows) <= 32

    def pack(self, source, target, relation, block):
        return (
            ((source - self.half) << self.source_at)
            + (target << self.target_at)
            + (relation << self.relation_at)
            + block
        )

    def bound(self, row):
        return (row - self.half) << self.source_at

    def source(self, word):
        return (word >> self.source_at) + self.half

    def target(self, word):
        return (word >> self.target_at) & ((1 << (self.source_at - self.target_at)) - 1)

    def relation(self, word):
        return (word >> self.relation_at) & ((1 << (self.target_at - self.relation_at)) - 1)

    def is_empty(self, word):
        return self.target(word) == (1 << (self.source_at - self.target_at)) - 1

    def block(self, word):
        return word & ((1 << self.relation_at) - 1)


def sort_columns(parts):
    count = len(parts)
    list_bits = bits_for(count)
    column = count * 8
    spread = max(1, TILE // column)
    low_lane_bits = bits_for(spread)
    lane_bits = [7 - low_lane_bits + k for k in range(low_lane_bits)] + list(range(7 - low_lane_bits))
    places = [("list", k) for k in range(list_bits)] + [("row", k) for k in range(3)] + [("lane", k) for k in lane_bits]
    row = lax.broadcasted_iota(jnp.int32, (8, 128), 0)
    lane = lax.broadcasted_iota(jnp.int32, (8, 128), 1)
    unset = {
        place: ((row if place[0] == "row" else lane) & (1 << place[1])) == 0
        for place in places
        if place[0] != "list"
    }
    total = len(places)

    def is_unset(index, position):
        if position == total:
            return True
        kind, bit = places[position]
        return index & (1 << bit) == 0 if kind == "list" else unset[(kind, bit)]

    def choose(mask, yes, no):
        if mask is True or mask is False:
            return yes if mask else no
        return jnp.where(mask, yes, no)

    for size in range(1, total + 1):
        for position in range(size - 1, -1, -1):
            kind, bit = places[position]
            if kind == "list":
                done = list(parts)
                for low in range(count):
                    high = low | 1 << bit
                    if high == low:
                        continue
                    up = is_unset(low, size)
                    small, large = jnp.minimum(parts[low], parts[high]), jnp.maximum(parts[low], parts[high])
                    done[low], done[high] = choose(up, small, large), choose(up, large, small)
                parts = done
                continue
            axis, extent = (0, 8) if kind == "row" else (1, 128)
            apart = 1 << bit
            first = unset[(kind, bit)]
            done = []
            for index, part in enumerate(parts):
                other = pltpu.roll(part, apart, axis)
                if 2 * apart != extent:
                    other = jnp.where(first, pltpu.roll(part, extent - apart, axis), other)
                small, large = jnp.minimum(part, other), jnp.maximum(part, other)
                up = is_unset(index, size)
                if up is True:
                    keep_small = first
                elif up is False:
                    keep_small = jnp.logical_not(first)
                else:
                    keep_small = jnp.logical_not(jnp.logical_xor(first, up))
                done.append(jnp.where(keep_small, small, large))
            parts = done
    return parts


def pick(table, place):
    out = jnp.int32(table[0])
    for at, entry in enumerate(table[1:], 1):
        out = jnp.where(place == at, jnp.int32(entry), out)
    return out


def open_kernel(tiles, share, place_ref, codes_hbm, scales_hbm, relations_hbm, edges_hbm, negatives_hbm, counts_hbm, *refs):
    reps = len(refs) - 11
    outs, refs = refs[:reps], refs[reps:]
    own_t_ref, values_t_ref, rel_t_ref, codes_ref, scales_ref, relations_ref, edges_ref, negatives_ref, counts_ref, counted, sems = refs
    place = place_ref[0]
    first = pl.multiple_of(place * share, 128)
    pairs = [
        (negatives_hbm, negatives_ref),
        (counts_hbm, counts_ref),
        (edges_hbm, edges_ref),
        (codes_hbm.at[pl.ds(first, share), :], codes_ref),
        (scales_hbm, scales_ref),
        (relations_hbm, relations_ref),
    ]
    copies = [pltpu.make_async_copy(source, target, sems.at[k]) for k, (source, target) in enumerate(pairs)]
    for copy in copies:
        copy.start()
    lanes = counted.shape[0]
    copies[0].wait()
    for block in range(tiles):
        negative = negatives_ref[block : block + 1, :]
        near = one_hot(LOW, negative & (LOW - 1))
        far = one_hot(lanes, negative >> (LOW.bit_length() - 1))
        held = nt_dot(far, near)
        for k in range(lanes):
            counted[k, block : block + 1, :] = held[k : k + 1, :]
    copies[1].wait()
    copies[2].wait()
    for apart, ids_ref in enumerate(outs):
        for tile in range(tiles):
            span = slice(tile * GROUP, (tile + 1) * GROUP)
            ids_ref[tile : tile + 1, :] = edges_ref[0:1, span] | (edges_ref[2:3, span] << 16)
        for tile in range(tiles // 2):
            near = edges_ref[1:2, tile * GROUP : (tile + 1) * GROUP]
            far = edges_ref[1:2, (tiles // 2 + tile) * GROUP : (tiles // 2 + tile + 1) * GROUP]
            ids_ref[tiles + tile : tiles + tile + 1, :] = near | (far << 16)
        to = place + apart
        to = jnp.where(to >= reps, to - reps, to)
        held = [counted[to * (share // LOW) + k] for k in range(share // LOW)]
        held += [jnp.zeros((tiles, GROUP - share), jnp.float32)] * (share < GROUP)
        held = jnp.concatenate(held, axis=1).astype(jnp.int32)
        ids_ref[3 * tiles // 2 : 2 * tiles, :] = held[: tiles // 2] | (held[tiles // 2 :] << 16)
        ids_ref[2 * tiles : 2 * tiles + 1, :] = jnp.full((1, GROUP), counts_ref[0], jnp.int32)
    for copy in copies[3:]:
        copy.wait()
    values_t = codes_ref[...].T.astype(jnp.float32) * scales_ref[:, pl.ds(first, share)].astype(jnp.float32)
    values_t_ref[...] = values_t
    own_t_ref[...] = values_t.astype(jnp.bfloat16)
    rel_t_ref[...] = relations_ref[...].T


def source_kernel(codes_ref, scales_ref, src_t_ref):
    codes_t = codes_ref[...].T.astype(jnp.float32)
    src_t_ref[...] = (codes_t * scales_ref[...].astype(jnp.float32)).astype(jnp.bfloat16)


def sort_kernel(packing, tiles, share, place_ref, *refs):
    ids_refs, (keys_ref, below_ref, ends_ref, ends_held, sem) = refs[:-5], refs[-5:]
    shards = len(ids_refs)
    first = place_ref[0] * share
    row = lax.broadcasted_iota(jnp.int32, (8, 128), 0)
    lane = lax.broadcasted_iota(jnp.int32, (8, 128), 1)
    keys, ranks, dead = [], [], jnp.zeros((1, 128), jnp.int32)
    for shard, ids_ref in enumerate(ids_refs):
        live = ids_ref[2 * tiles : 2 * tiles + 1, 0:128]
        relations = unpack(ids_ref[tiles : 3 * tiles // 2, :])
        for top in range(0, tiles, 8):
            for left in range(0, GROUP, 128):
                word = ids_ref[top : top + 8, left : left + 128]
                relation = relations[top : top + 8, left : left + 128]
                target = (word >> 16) - first
                target = jnp.where((target >= 0) & (target < share), target, share)
                key = packing.pack(word & 0xFFFF, target, relation, shard * tiles + top + row)
                over = (top + row) * GROUP + left + lane - live
                keys.append(jnp.where(over < 0, key, LAST_KEY))
                ranks.append(jnp.where(over < 0, LAST_KEY, over + dead))
        dead = dead + (tiles * GROUP - live)
    below = [jnp.int32(0)]
    for at in range(1, shards + 1):
        bound = LAST_KEY if at == shards else packing.bound(at * share)
        inside = functools.reduce(jnp.add, [jnp.where(key < bound, 1.0, 0.0) for key in keys])
        below.append(jnp.sum(inside).astype(jnp.int32))
    fill = [(below[at] - below[at + 1]) & (TILE - 1) for at in range(shards)]
    enough = functools.reduce(jnp.add, fill) <= len(keys) * 1024 - below[-1]
    filled = [jnp.int32(0)]
    for at in range(shards):
        filled.append(filled[at] + jnp.where(enough, fill[at], 0))
    for at in range(shards + 1):
        below_ref[at] = below[at] + filled[at]
    parts = []
    for key, rank in zip(keys, ranks):
        for at in range(shards - 2, -1, -1):
            key = jnp.where(rank < filled[at + 1], packing.bound((at + 1) * share) - 1, key)
        parts.append(key)
    parts = sort_columns(parts)
    ends_held[...] = jnp.zeros_like(ends_held)
    ends_held[0:1, :] = parts[0][0:1, :]
    ends_held[1:2, :] = parts[-1][7:8, :]
    copy = pltpu.make_async_copy(ends_held, ends_ref, sem)
    copy.start()
    columns = jnp.concatenate(parts, axis=0).T
    spread = max(1, TILE // columns.shape[1])
    rows = columns.shape[0] // spread
    for k in range(spread):
        keys_ref[:rows, k * columns.shape[1] : (k + 1) * columns.shape[1]] = columns[k * rows : (k + 1) * rows]
    keys_ref[rows:, :] = jnp.full((keys_ref.shape[0] - rows, TILE), LAST_KEY, jnp.int32)
    copy.wait()


def part_kernel(packing, tables, opening, closing, negs, place_ref, below_ref, ends_ref, keys_ref, src_t_ref, rel_t_ref, dst_t_ref, *refs):
    refs = list(refs)
    src_total = refs.pop()
    if closing:
        *refs, coef_ref, query_ref, relation_ref, new_query_ref, new_relation_ref, dst_total = refs
        half_ref, times_ref, before_ref, *given, after_ref, src_grad_ref, dst_grad_ref, coefs_ref = refs
        dst_total[...] = before_ref[...]
        for held, source in zip((coef_ref, query_ref, relation_ref, new_query_ref, new_relation_ref), given):
            held[...] = source[...]
    elif opening:
        *ids_refs, src_grad_ref, dst_total, coef_ref, query_ref, relation_ref, new_query_ref, new_relation_ref, half_ref, times_ref = refs
        half_ref[...] = dst_t_ref[...].T * jnp.bfloat16(0.5)
        tiles = ids_refs[0].shape[0] // 2
        counted = [unpack(ids_ref[3 * tiles // 2 : 2 * tiles, : half_ref.shape[0]]) for ids_ref in ids_refs]
        counted = jnp.concatenate(counted, axis=0).astype(jnp.float32) * (0.5 / negs)
        times_ref[...] = counted.T.astype(times_ref.dtype)
        dst_total[...] = jnp.zeros_like(dst_total)
    else:
        half_ref, times_ref = refs[:2]
        src_grad_ref, dst_total, coef_ref, query_ref, relation_ref, new_query_ref, new_relation_ref = refs[-7:]
    share, width = half_ref.shape

    def span(table):
        at = pick(table, place_ref[0])
        start = pl.multiple_of(at * share, 128)
        begin = below_ref[at] // TILE
        return start, begin, jnp.maximum((below_ref[at + 1] + TILE - 1) // TILE, begin + 1)

    spans = [span(table) for table in tables]
    spans = spans + spans[-1:] * (3 - len(spans))
    start, begin, end = spans[0]
    src_total[...] = jnp.zeros_like(src_total)
    last_row = keys_ref.shape[0] - 9

    def after(at):
        (_, _, end0), (start1, begin1, end1), (start2, begin2, _) = spans
        over, soon, over1 = at + 1 >= end0, at + 2 >= end0, begin1 + 1 >= end1
        one = jnp.where(over, begin1, at + 1)
        two = jnp.where(over, jnp.where(over1, begin2, begin1 + 1), jnp.where(soon, begin1, at + 2))
        two_start = jnp.where(over, jnp.where(over1, start2, start1), jnp.where(soon, start1, start))
        return one, two, pl.multiple_of(two_start, 128)

    def word_of(at):
        return keys_ref[pl.ds(at, 1), :]

    def window(at, start):
        at = jnp.minimum(at, last_row)
        low = packing.source(ends_ref[0, at]) - start
        high = packing.source(ends_ref[1, at + 127 - last_row]) - start
        low = jnp.clip((low >> 7) << 7, 0, share - NARROW)
        return pl.multiple_of(low, 128), jnp.minimum(high, share - 1) - low < NARROW

    def sources(word, start, extent):
        return one_hot(extent, jnp.where(packing.is_empty(word), -1, packing.source(word) - start))

    def query_of(word, start, extent):
        relation = nn_dot(rel_t_ref[...], one_hot(rel_t_ref.shape[1], packing.relation(word)))
        relation = relation.astype(jnp.bfloat16)
        found = nn_dot(src_t_ref[:, pl.ds(start, extent)], sources(word, start, extent))
        return found.astype(jnp.bfloat16) * relation, relation

    def coef_of(word, query):
        times = nn_dot(times_ref[...], one_hot(times_ref.shape[1], packing.block(word))).astype(jnp.bfloat16)
        bend = jnp.tanh(nn_dot(half_ref[...], query))
        below = (bend - 1.0).astype(jnp.bfloat16)
        return times * (bend + 1.0).astype(jnp.bfloat16) + one_hot(share, packing.target(word), 0.5) * below

    def keep(coef, query, relation, new_query, new_relation):
        coef_ref[...] = coef
        query_ref[...] = query
        relation_ref[...] = relation
        new_query_ref[...] = new_query
        new_relation_ref[...] = new_relation

    if opening:
        query, relation = query_of(word_of(begin), start, share)
        one, _, _ = after(begin)
        one_start = pl.multiple_of(jnp.where(begin + 1 >= end, spans[1][0], start), 128)
        new_query, new_relation = query_of(word_of(one), one_start, share)
        keep(coef_of(word_of(begin), query), query, relation, new_query, new_relation)

    def work(at, one, two, low, two_from, extent):
        coef, query, relation = coef_ref[...], query_ref[...], relation_ref[...]
        new_query, new_relation = new_query_ref[...], new_relation_ref[...]
        back = nn_dot(dst_t_ref[...], coef)
        third_query, third_relation = query_of(word_of(two), two_from, extent)
        new_coef = coef_of(word_of(one), new_query)
        dst_total[...] += nt_dot(coef, query)
        back = back.astype(jnp.bfloat16) * relation
        src_total[pl.ds(low, extent), :] += nt_dot(sources(word_of(at), start + low, extent), back)
        keep(new_coef, new_query, new_relation, third_query, third_relation)

    def light_work(at, one, two, low, two_from, extent):
        coef, query = coef_ref[...], query_ref[...]
        new_query, new_relation = new_query_ref[...], new_relation_ref[...]
        third_query, third_relation = query_of(word_of(two), two_from, extent)
        new_coef = coef_of(word_of(one), new_query)
        dst_total[...] += nt_dot(coef, query)
        coefs_ref[at - begin] = coef
        keep(new_coef, new_query, new_relation, third_query, third_relation)

    def step_with(work):
        def step(at, carry):
            one, two, two_start = after(at)
            if share <= NARROW:
                work(at, one, two, 0, two_start, share)
                return carry
            low, fits = window(at, start)
            two_low, two_fits = window(two, two_start)
            narrow = jnp.logical_and(fits, two_fits)

            @pl.when(narrow)
            def _():
                work(at, one, two, low, pl.multiple_of(two_start + two_low, 128), NARROW)

            @pl.when(jnp.logical_not(narrow))
            def _():
                work(at, one, two, 0, two_start, share)

            return carry

        return step

    light = begin
    if closing:
        light = jnp.minimum(end, begin + HELD)
        lax.fori_loop(begin, light, step_with(light_work), 0)
    lax.fori_loop(light, end, step_with(work), 0)
    src_grad_ref[...] = src_total[...].astype(src_grad_ref.dtype)
    if closing:
        dst_grad_ref[...] = dst_total[...].astype(dst_grad_ref.dtype)


def finish_kernel(packing, owners, place_ref, below_ref, keys_ref, src_grad_ref, rel_t_ref, dst_t_ref, coefs_ref, own_ref, src_total):
    share = own_ref.shape[0]
    at = pick(owners, place_ref[0])
    start = at * share
    begin = below_ref[at] // TILE
    end = jnp.maximum((below_ref[at + 1] + TILE - 1) // TILE, begin + 1)
    src_total[...] = src_grad_ref[...]

    def step(at, carry):
        word = keys_ref[pl.ds(at, 1), :]
        relation = nn_dot(rel_t_ref[...], one_hot(rel_t_ref.shape[1], packing.relation(word)))
        back = (nn_dot(dst_t_ref[...], coefs_ref[at - begin]) * relation).astype(jnp.bfloat16)
        source = one_hot(share, jnp.where(packing.is_empty(word), -1, packing.source(word) - start))
        src_total[...] += nt_dot(source, back)
        return carry

    lax.fori_loop(begin, jnp.minimum(end, begin + HELD), step, 0)
    own_ref[...] = src_total[...].astype(own_ref.dtype)


def update_kernel(place_ref, values_t_ref, scales_ref, accum_ref, arrived_ref, own_ref, returned_ref, piece_ref, low_ref, high_ref, state_ref):
    share = arrived_ref.shape[0]
    first = pl.multiple_of(place_ref[0] * share, 128)
    summed = arrived_ref[...].astype(jnp.float32) + own_ref[...].astype(jnp.float32)
    summed = (summed + returned_ref[...].astype(jnp.float32)).T
    scale = scales_ref[:, pl.ds(first, share)].astype(jnp.float32)
    state = accum_ref[:, pl.ds(first, share)] + jnp.mean(summed * summed, axis=0, keepdims=True)
    updated = values_t_ref[...] - summed * (LEARN_RATE / (jnp.sqrt(state) + ROOT_EPSILON))
    piece = (updated * (1.0 / scale)).T.astype(piece_ref.dtype)
    piece_ref[...] = piece
    low_ref[...] = piece[: share // 2]
    high_ref[...] = piece[share // 2 :]
    state_ref[...] = state


def place_kernel(tables, unit, place_ref, *refs):
    pieces, (out_ref, sems) = refs[: len(tables)], refs[-2:]
    place = place_ref[0]
    copies = []
    for k, (table, chosen) in enumerate(tables):
        row = pl.multiple_of(pick(table, place) * unit, 128)
        copies.append(pltpu.make_async_copy(pieces[k], out_ref.at[pl.ds(row, pieces[k].shape[0]), :], sems.at[k]))
    for act in ("start", "wait"):
        for copy, (_, chosen) in zip(copies, tables):
            if chosen is None:
                getattr(copy, act)()
            else:
                pl.when(pick(chosen, place) == 1)(getattr(copy, act))


SMEM = pl.BlockSpec(memory_space=pltpu.SMEM)
VMEM = pl.BlockSpec(memory_space=pltpu.VMEM)


ANY = pl.BlockSpec(memory_space=pl.ANY)
HBM = pl.BlockSpec(memory_space=pltpu.HBM)


def call(kernel, inputs, outs, scratch, name, us, scalars=1, unread=0, aliases={}, scalar_outs=(), in_hbm=0, out=None, grant=VMEM_LIMIT):
    return pl.pallas_call(
        kernel,
        out_shape=outs,
        in_specs=[SMEM] * scalars + [HBM] * in_hbm + [VMEM] * (len(inputs) - scalars - in_hbm - unread) + [ANY] * unread,
        out_specs=out or ([SMEM if at in scalar_outs else VMEM for at in range(len(outs))] if isinstance(outs, tuple) else VMEM),
        scratch_shapes=scratch,
        input_output_aliases=aliases,
        compiler_params=pltpu.CompilerParams(vmem_limit_bytes=grant),
        cost_estimate=pl.CostEstimate(flops=int(us * 1.15e9), bytes_accessed=0, transcendentals=0),
        name=name,
    )(*inputs)


def body(codes, scales, accum, relations, matching, edges, counts, negatives):
    reps = lax.axis_size("rep")
    at_rep = lax.axis_index("rep")
    place = at_rep[None]
    apart_dom = jnp.bitwise_xor(matching[0], lax.axis_index("dom"))
    part_rows, width = codes.shape
    slots = edges.shape[1]
    tiles = slots // GROUP
    negs = negatives.shape[1]
    share = part_rows // reps
    scales_row, accum_row = scales[None], accum[None]

    shape = jax.ShapeDtypeStruct
    ids_shape = shape((2 * tiles + 1, GROUP), jnp.int32)
    *sent, own_t, values_t, rel_t = call(
        functools.partial(open_kernel, tiles, share),
        (place, codes, scales_row, relations, edges, negatives, counts),
        (ids_shape,) * reps
        + (shape((width, share), jnp.bfloat16), shape((width, share), jnp.float32),
           shape(relations.shape[::-1], jnp.bfloat16)),
        [pltpu.VMEM((share, width), codes.dtype), pltpu.VMEM(scales_row.shape, scales.dtype),
         pltpu.VMEM(relations.shape, relations.dtype), pltpu.VMEM(edges.shape, edges.dtype),
         pltpu.VMEM(negatives.shape, negatives.dtype), pltpu.SMEM(counts.shape, counts.dtype),
         pltpu.VMEM((part_rows // LOW, tiles, LOW), jnp.float32), pltpu.SemaphoreType.DMA((6,))],
        "open", 3, in_hbm=6, grant=56 * 1024 * 1024)

    part = shape((share, width), jnp.bfloat16)
    part_sum = shape((share, width), jnp.float32)
    total = pltpu.VMEM((share, width), jnp.float32)
    packing = Packing(part_rows, share, relations.shape[0], reps * tiles)

    @jax.jit
    def sort_edges(place, *ids):
        return call(
            functools.partial(sort_kernel, packing, tiles, share), (place, *ids),
            (shape((reps * slots // TILE + 8, TILE), jnp.int32), shape((reps + 1,), jnp.int32),
             shape((8, 128), jnp.int32)),
            [pltpu.VMEM((8, 128), jnp.int32), pltpu.SemaphoreType.DMA], "sort", 5, scalar_outs=(1, 2))

    def gather_edges(place, codes, scales_row, *sent):
        ids = [sent[0]]
        for apart in range(1, reps):
            along = [(at, (at + apart) % reps) for at in range(reps)]
            ids.append(lax.ppermute(sent[apart], "rep", along))
        src_t = call(source_kernel, (codes, scales_row), shape((width, part_rows), jnp.bfloat16), [], "source", 2, scalars=0)
        return (src_t, *ids) + tuple(sort_edges(place, *ids))

    dst_t, src_t, *ids, keys, below, ends = swap_beside(
        apart_dom, own_t, gather_edges, place, codes, scales_row, *sent)

    order = ring_order(reps)
    forward = [(order[i], order[(i + 1) % reps]) for i in range(reps)]

    def owners(behind):
        return [order[(order.index(z) - behind) % reps] for z in range(reps)]

    wide = shape((share, TILE), jnp.bfloat16)
    tall = shape((width, TILE), jnp.bfloat16)
    state = [wide, tall, tall, tall, tall]
    moving = arrived = None
    for behind in range(1, reps + 1):
        opening, closing = behind == 1, behind == reps
        table = owners(behind)
        chain = [owners(later) for later in range(behind, min(behind + 2, reps) + 1)]
        kept = shape((HELD, share, TILE), jnp.bfloat16)
        outs = (part_sum, part, kept) if closing else (part, part_sum, *state)
        scratch = ([pltpu.VMEM(kept.shape, kept.dtype) for kept in state] + [total] if closing else []) + [total]
        if opening:
            given = tuple(ids)
            outs += (part, shape((share, reps * tiles), jnp.bfloat16))
        else:
            given = (half, times, dst_grad) + held + (arrived if arrived is not None else below,)
        done = call(
            functools.partial(part_kernel, packing, chain, opening, closing, negs),
            (place, below, ends, keys, src_t, rel_t, dst_t) + given, outs, scratch, "part", 9,
            scalars=3, unread=0 if opening else 1,
            aliases={} if opening or closing else {9 + k: 1 + k for k in range(6)})
        src_grad, dst_grad = done[:2]
        held = tuple(done[2:7])
        if opening:
            half, times = done[7:]
            moving = src_grad
        elif not closing:
            arrived = lax.ppermute(moving, "rep", forward)
            moving = (arrived.astype(jnp.float32) + src_grad.astype(jnp.float32)).astype(jnp.bfloat16)
    arrived = lax.ppermute(moving, "rep", forward)
    @jax.jit
    def finish(*given):
        return call(functools.partial(finish_kernel, packing, table), given, part, [total], "finish", 3, scalars=2)

    returned, own = swap_beside(
        apart_dom, dst_grad, lambda *given: (finish(*given),), place, below, keys, src_grad, rel_t, dst_t, done[2])

    half_part = shape((share // 2, width), jnp.bfloat16)
    piece, low, high, state = call(
        update_kernel, (place, values_t, scales_row, accum_row, arrived, own, returned),
        (part, half_part, half_part, shape((1, share), jnp.float32)), [], "update", 2)

    def put(tables, pieces, given, us):
        return call(
            functools.partial(place_kernel, tables, share // 2), (place, *pieces) + given, shape(codes.shape, jnp.bfloat16),
            [pltpu.SemaphoreType.DMA((len(pieces),))], "place", us, unread=len(given),
            aliases={1 + len(pieces): 0} if given else {}, out=HBM)

    if reps == 4:
        across = [(0, 2), (2, 0), (1, 3), (3, 1)]
        far = [lax.ppermute(held, "rep", across) for held in (low, high)]
        near = lax.ppermute(piece, "rep", [(0, 1), (1, 0), (2, 3), (3, 2)])
        middle = lax.ppermute(piece, "rep", [(1, 2), (2, 1)])
        ends = [lax.ppermute(held, "rep", [(2, 3), (1, 0)]) for held in far]
        early = [(piece, ([0, 2, 4, 6], None)), (near, ([2, 0, 6, 4], None))]
        early += [(held, ([4 + k, 6 + k, k, 2 + k], None)) for k, held in enumerate(far)]
        late = [(middle, ([6, 4, 2, 0], [0, 1, 1, 0]))]
        late += [(held, ([6 + k, 4 + k, 2 + k, k], [1, 0, 0, 1])) for k, held in enumerate(ends)]
    else:
        pieces = [piece]
        for behind in range(1, reps):
            pieces.append(lax.ppermute(pieces[-1], "rep", forward))
        early = [(held, ([2 * at for at in owners(behind)], None)) for behind, held in enumerate(pieces)]
        early, late = early[:-1], early[-1:]
    new_codes = put([table for _, table in early], [held for held, _ in early], (), 1)
    new_codes = put([table for _, table in late], [held for held, _ in late], (new_codes,), 1)
    return (new_codes, state[0])


def solution(mesh):
    placed = (
        P("dom", None),
        P("dom"),
        P("dom"),
        P(),
        P("dom"),
        P(None, ("dom", "rep")),
        P(("dom", "rep")),
        P(("dom", "rep"), None),
    )
    return jax.shard_map(
        body,
        mesh=mesh,
        in_specs=placed,
        out_specs=(P("dom", None), P(("dom", "rep"))),
        check_vma=False,
    )
```

```python
import functools

import jax
import jax.numpy as jnp
from jax import lax
from jax.experimental import pallas as pl
from jax.experimental.pallas import tpu as pltpu
from jax.sharding import PartitionSpec as P

GROUP = 512
LOW = 128
TILE = 512
NARROW = 256
HELD = 10
LAST_KEY = 2**31 - 1
LEARN_RATE = 0.1
ROOT_EPSILON = 1e-08
VMEM_LIMIT = 24 * 1024 * 1024


def swap_beside(apart, block, beside, *args):
    count = lax.axis_size("dom")

    def route(bits):
        return [(at, at ^ bits) for at in range(count)]

    if count <= 8:

        def branch(bits):
            return lambda block, *args: (lax.ppermute(block, "dom", route(bits)),) + beside(*args)

        return lax.switch(apart - 1, [branch(bits) for bits in range(1, count)], block, *args)
    for bit in range(count.bit_length() - 1):
        here = jnp.bitwise_and(jnp.right_shift(apart, bit), 1) == 1
        block = lax.cond(here, lambda b: lax.ppermute(b, "dom", route(1 << bit)), lambda b: b, block)
    return (block,) + beside(*args)


def ring_order(count):
    return list(range(0, count, 2)) + list(range(1, count, 2))[::-1]


def one_hot(rows, ids, one=1):
    step = min(rows, 256)
    spots = lax.broadcasted_iota(jnp.int32, (step, ids.shape[1]), 0).astype(jnp.bfloat16)
    low = (ids & (step - 1)).astype(jnp.float32)
    parts = []
    for first in range(0, rows, step):
        inside = (ids >= first) & (ids < first + step)
        key = jnp.where(inside, low, -1.0).astype(jnp.bfloat16)
        parts.append(jnp.where(spots == key, jnp.bfloat16(one), jnp.bfloat16(0)))
    return jnp.concatenate(parts, axis=0) if len(parts) > 1 else parts[0]


def nt_dot(a, b):
    return lax.dot_general(a, b, (((1,), (1,)), ((), ())), preferred_element_type=jnp.float32)


def nn_dot(a, b):
    return jnp.dot(a, b, preferred_element_type=jnp.float32)


def unpack(words):
    return jnp.concatenate([words & 0xFFFF, words >> 16], axis=0)


def bits_for(count):
    return (count - 1).bit_length()


class Packing:
    def __init__(self, part_rows, share, relations, blocks):
        self.half = part_rows // 2
        self.relation_at = bits_for(blocks)
        self.target_at = self.relation_at + bits_for(relations)
        self.source_at = self.target_at + bits_for(share + 1)
        assert self.source_at + bits_for(part_rows) <= 32

    def pack(self, source, target, relation, block):
        return (
            ((source - self.half) << self.source_at)
            + (target << self.target_at)
            + (relation << self.relation_at)
            + block
        )

    def bound(self, row):
        return (row - self.half) << self.source_at

    def source(self, word):
        return (word >> self.source_at) + self.half

    def target(self, word):
        return (word >> self.target_at) & ((1 << (self.source_at - self.target_at)) - 1)

    def relation(self, word):
        return (word >> self.relation_at) & ((1 << (self.target_at - self.relation_at)) - 1)

    def is_empty(self, word):
        return self.target(word) == (1 << (self.source_at - self.target_at)) - 1

    def block(self, word):
        return word & ((1 << self.relation_at) - 1)


def sort_columns(parts):
    count = len(parts)
    list_bits = bits_for(count)
    column = count * 8
    spread = max(1, TILE // column)
    low_lane_bits = bits_for(spread)
    lane_bits = [7 - low_lane_bits + k for k in range(low_lane_bits)] + list(range(7 - low_lane_bits))
    places = [("list", k) for k in range(list_bits)] + [("row", k) for k in range(3)] + [("lane", k) for k in lane_bits]
    row = lax.broadcasted_iota(jnp.int32, (8, 128), 0)
    lane = lax.broadcasted_iota(jnp.int32, (8, 128), 1)
    unset = {
        place: ((row if place[0] == "row" else lane) & (1 << place[1])) == 0
        for place in places
        if place[0] != "list"
    }
    total = len(places)

    def is_unset(index, position):
        if position == total:
            return True
        kind, bit = places[position]
        return index & (1 << bit) == 0 if kind == "list" else unset[(kind, bit)]

    def choose(mask, yes, no):
        if mask is True or mask is False:
            return yes if mask else no
        return jnp.where(mask, yes, no)

    for size in range(1, total + 1):
        for position in range(size - 1, -1, -1):
            kind, bit = places[position]
            if kind == "list":
                done = list(parts)
                for low in range(count):
                    high = low | 1 << bit
                    if high == low:
                        continue
                    up = is_unset(low, size)
                    small, large = jnp.minimum(parts[low], parts[high]), jnp.maximum(parts[low], parts[high])
                    done[low], done[high] = choose(up, small, large), choose(up, large, small)
                parts = done
                continue
            axis, extent = (0, 8) if kind == "row" else (1, 128)
            apart = 1 << bit
            first = unset[(kind, bit)]
            done = []
            for index, part in enumerate(parts):
                other = pltpu.roll(part, apart, axis)
                if 2 * apart != extent:
                    other = jnp.where(first, pltpu.roll(part, extent - apart, axis), other)
                small, large = jnp.minimum(part, other), jnp.maximum(part, other)
                up = is_unset(index, size)
                if up is True:
                    keep_small = first
                elif up is False:
                    keep_small = jnp.logical_not(first)
                else:
                    keep_small = jnp.logical_not(jnp.logical_xor(first, up))
                done.append(jnp.where(keep_small, small, large))
            parts = done
    return parts


def pick(table, place):
    out = jnp.int32(table[0])
    for at, entry in enumerate(table[1:], 1):
        out = jnp.where(place == at, jnp.int32(entry), out)
    return out


def open_kernel(tiles, share, place_ref, codes_hbm, scales_hbm, relations_hbm, edges_hbm, negatives_hbm, counts_hbm, *refs):
    refs, wide_scales = refs[:-1], refs[-1]
    reps = len(refs) - 11
    outs, refs = refs[:reps], refs[reps:]
    own_t_ref, values_t_ref, rel_t_ref, codes_ref, scales_ref, relations_ref, edges_ref, negatives_ref, counts_ref, counted, sems = refs
    place = place_ref[0]
    first = pl.multiple_of(place * share, 128)
    pairs = [
        (negatives_hbm, negatives_ref),
        (counts_hbm, counts_ref),
        (edges_hbm, edges_ref),
        (codes_hbm.at[pl.ds(first, share), :], codes_ref),
        (scales_hbm, scales_ref),
        (relations_hbm, relations_ref),
    ]
    copies = [pltpu.make_async_copy(source, target, sems.at[k]) for k, (source, target) in enumerate(pairs)]
    for copy in copies:
        copy.start()
    lanes = counted.shape[0]
    copies[0].wait()
    for block in range(tiles):
        negative = negatives_ref[block : block + 1, :]
        near = one_hot(LOW, negative & (LOW - 1))
        far = one_hot(lanes, negative >> (LOW.bit_length() - 1))
        held = nt_dot(far, near)
        for k in range(lanes):
            counted[k, block : block + 1, :] = held[k : k + 1, :]
    copies[1].wait()
    copies[2].wait()
    for apart, ids_ref in enumerate(outs):
        for tile in range(tiles):
            span = slice(tile * GROUP, (tile + 1) * GROUP)
            ids_ref[tile : tile + 1, :] = edges_ref[0:1, span] | (edges_ref[2:3, span] << 16)
        for tile in range(tiles // 2):
            near = edges_ref[1:2, tile * GROUP : (tile + 1) * GROUP]
            far = edges_ref[1:2, (tiles // 2 + tile) * GROUP : (tiles // 2 + tile + 1) * GROUP]
            ids_ref[tiles + tile : tiles + tile + 1, :] = near | (far << 16)
        to = place + apart
        to = jnp.where(to >= reps, to - reps, to)
        held = [counted[to * (share // LOW) + k] for k in range(share // LOW)]
        held += [jnp.zeros((tiles, GROUP - share), jnp.float32)] * (share < GROUP)
        held = jnp.concatenate(held, axis=1).astype(jnp.int32)
        ids_ref[3 * tiles // 2 : 2 * tiles, :] = held[: tiles // 2] | (held[tiles // 2 :] << 16)
        ids_ref[2 * tiles : 2 * tiles + 1, :] = jnp.full((1, GROUP), counts_ref[0], jnp.int32)
    for copy in copies[3:]:
        copy.wait()
    wide_scales[...] = scales_ref[...].astype(jnp.float32)
    values_t = codes_ref[...].T.astype(jnp.float32) * scales_of(wide_scales, first, share)
    values_t_ref[...] = values_t
    own_t_ref[...] = values_t.astype(jnp.bfloat16)
    rel_t_ref[...] = relations_ref[...].T


def scales_of(rows_ref, first, count):
    rows = [rows_ref[pl.ds(first // 128 + k, 1), :] for k in range(count // 128)]
    return jnp.concatenate(rows, axis=1)


def source_kernel(codes_ref, scales_ref, src_t_ref, wide_scales):
    codes_t = codes_ref[...].T.astype(jnp.float32)
    wide_scales[...] = scales_ref[...].astype(jnp.float32)
    src_t_ref[...] = (codes_t * scales_of(wide_scales, 0, codes_ref.shape[0])).astype(jnp.bfloat16)


def sort_kernel(packing, tiles, share, place_ref, *refs):
    ids_refs, (keys_ref, below_ref, ends_ref, ends_held, sem) = refs[:-5], refs[-5:]
    shards = len(ids_refs)
    first = place_ref[0] * share
    row = lax.broadcasted_iota(jnp.int32, (8, 128), 0)
    lane = lax.broadcasted_iota(jnp.int32, (8, 128), 1)
    keys, ranks, dead = [], [], jnp.zeros((1, 128), jnp.int32)
    for shard, ids_ref in enumerate(ids_refs):
        live = ids_ref[2 * tiles : 2 * tiles + 1, 0:128]
        relations = unpack(ids_ref[tiles : 3 * tiles // 2, :])
        for top in range(0, tiles, 8):
            for left in range(0, GROUP, 128):
                word = ids_ref[top : top + 8, left : left + 128]
                relation = relations[top : top + 8, left : left + 128]
                target = (word >> 16) - first
                target = jnp.where((target >= 0) & (target < share), target, share)
                key = packing.pack(word & 0xFFFF, target, relation, shard * tiles + top + row)
                over = (top + row) * GROUP + left + lane - live
                keys.append(jnp.where(over < 0, key, LAST_KEY))
                ranks.append(jnp.where(over < 0, LAST_KEY, over + dead))
        dead = dead + (tiles * GROUP - live)
    below = [jnp.int32(0)]
    for at in range(1, shards + 1):
        bound = LAST_KEY if at == shards else packing.bound(at * share)
        inside = functools.reduce(jnp.add, [jnp.where(key < bound, 1.0, 0.0) for key in keys])
        below.append(jnp.sum(inside).astype(jnp.int32))
    fill = [(below[at] - below[at + 1]) & (TILE - 1) for at in range(shards)]
    enough = functools.reduce(jnp.add, fill) <= len(keys) * 1024 - below[-1]
    filled = [jnp.int32(0)]
    for at in range(shards):
        filled.append(filled[at] + jnp.where(enough, fill[at], 0))
    for at in range(shards + 1):
        below_ref[at] = below[at] + filled[at]
    parts = []
    for key, rank in zip(keys, ranks):
        for at in range(shards - 2, -1, -1):
            key = jnp.where(rank < filled[at + 1], packing.bound((at + 1) * share) - 1, key)
        parts.append(key)
    parts = sort_columns(parts)
    ends_held[...] = jnp.zeros_like(ends_held)
    ends_held[0:1, :] = parts[0][0:1, :]
    ends_held[1:2, :] = parts[-1][7:8, :]
    copy = pltpu.make_async_copy(ends_held, ends_ref, sem)
    copy.start()
    columns = jnp.concatenate(parts, axis=0).T
    spread = max(1, TILE // columns.shape[1])
    rows = columns.shape[0] // spread
    for k in range(spread):
        keys_ref[:rows, k * columns.shape[1] : (k + 1) * columns.shape[1]] = columns[k * rows : (k + 1) * rows]
    keys_ref[rows:, :] = jnp.full((keys_ref.shape[0] - rows, TILE), LAST_KEY, jnp.int32)
    copy.wait()


def part_kernel(packing, tables, opening, closing, negs, place_ref, below_ref, ends_ref, keys_ref, src_t_ref, rel_t_ref, dst_t_ref, *refs):
    refs = list(refs)
    src_total = refs.pop()
    if closing:
        *refs, coef_ref, query_ref, relation_ref, new_query_ref, new_relation_ref, dst_total = refs
        half_ref, times_ref, before_ref, *given, after_ref, src_grad_ref, dst_grad_ref, coefs_ref = refs
        dst_total[...] = before_ref[...]
        for held, source in zip((coef_ref, query_ref, relation_ref, new_query_ref, new_relation_ref), given):
            held[...] = source[...]
    elif opening:
        *ids_refs, src_grad_ref, dst_total, coef_ref, query_ref, relation_ref, new_query_ref, new_relation_ref, half_ref, times_ref = refs
        half_ref[...] = dst_t_ref[...].T * jnp.bfloat16(0.5)
        tiles = ids_refs[0].shape[0] // 2
        counted = [unpack(ids_ref[3 * tiles // 2 : 2 * tiles, : half_ref.shape[0]]) for ids_ref in ids_refs]
        counted = jnp.concatenate(counted, axis=0).astype(jnp.float32) * (0.5 / negs)
        times_ref[...] = counted.T.astype(times_ref.dtype)
        dst_total[...] = jnp.zeros_like(dst_total)
    else:
        half_ref, times_ref = refs[:2]
        src_grad_ref, dst_total, coef_ref, query_ref, relation_ref, new_query_ref, new_relation_ref = refs[-7:]
    share, width = half_ref.shape

    def span(table):
        at = pick(table, place_ref[0])
        start = pl.multiple_of(at * share, 128)
        begin = below_ref[at] // TILE
        return start, begin, jnp.maximum((below_ref[at + 1] + TILE - 1) // TILE, begin + 1)

    spans = [span(table) for table in tables]
    spans = spans + spans[-1:] * (3 - len(spans))
    start, begin, end = spans[0]
    src_total[...] = jnp.zeros_like(src_total)
    last_row = keys_ref.shape[0] - 9

    def after(at):
        (_, _, end0), (start1, begin1, end1), (start2, begin2, _) = spans
        over, soon, over1 = at + 1 >= end0, at + 2 >= end0, begin1 + 1 >= end1
        one = jnp.where(over, begin1, at + 1)
        two = jnp.where(over, jnp.where(over1, begin2, begin1 + 1), jnp.where(soon, begin1, at + 2))
        two_start = jnp.where(over, jnp.where(over1, start2, start1), jnp.where(soon, start1, start))
        return one, two, pl.multiple_of(two_start, 128)

    def word_of(at):
        return keys_ref[pl.ds(at, 1), :]

    def window(at, start):
        at = jnp.minimum(at, last_row)
        low = packing.source(ends_ref[0, at]) - start
        high = packing.source(ends_ref[1, at + 127 - last_row]) - start
        low = jnp.clip((low >> 7) << 7, 0, share - NARROW)
        return pl.multiple_of(low, 128), jnp.minimum(high, share - 1) - low < NARROW

    def sources(word, start, extent):
        return one_hot(extent, jnp.where(packing.is_empty(word), -1, packing.source(word) - start))

    def query_of(word, start, extent):
        relation = nn_dot(rel_t_ref[...], one_hot(rel_t_ref.shape[1], packing.relation(word)))
        relation = relation.astype(jnp.bfloat16)
        found = nn_dot(src_t_ref[:, pl.ds(start, extent)], sources(word, start, extent))
        return found.astype(jnp.bfloat16) * relation, relation

    def coef_of(word, query):
        times = nn_dot(times_ref[...], one_hot(times_ref.shape[1], packing.block(word))).astype(jnp.bfloat16)
        bend = jnp.tanh(nn_dot(half_ref[...], query))
        below = (bend - 1.0).astype(jnp.bfloat16)
        return times * (bend + 1.0).astype(jnp.bfloat16) + one_hot(share, packing.target(word), 0.5) * below

    def keep(coef, query, relation, new_query, new_relation):
        coef_ref[...] = coef
        query_ref[...] = query
        relation_ref[...] = relation
        new_query_ref[...] = new_query
        new_relation_ref[...] = new_relation

    if opening:
        query, relation = query_of(word_of(begin), start, share)
        one, _, _ = after(begin)
        one_start = pl.multiple_of(jnp.where(begin + 1 >= end, spans[1][0], start), 128)
        new_query, new_relation = query_of(word_of(one), one_start, share)
        keep(coef_of(word_of(begin), query), query, relation, new_query, new_relation)

    def work(at, one, two, low, two_from, extent):
        coef, query, relation = coef_ref[...], query_ref[...], relation_ref[...]
        new_query, new_relation = new_query_ref[...], new_relation_ref[...]
        new_coef = coef_of(word_of(one), new_query)
        back = nn_dot(dst_t_ref[...], coef)
        third_query, third_relation = query_of(word_of(two), two_from, extent)
        dst_total[...] += nt_dot(coef, query)
        back = back.astype(jnp.bfloat16) * relation
        src_total[pl.ds(low, extent), :] += nt_dot(sources(word_of(at), start + low, extent), back)
        keep(new_coef, new_query, new_relation, third_query, third_relation)

    def light_work(at, one, two, low, two_from, extent):
        coef, query = coef_ref[...], query_ref[...]
        new_query, new_relation = new_query_ref[...], new_relation_ref[...]
        new_coef = coef_of(word_of(one), new_query)
        third_query, third_relation = query_of(word_of(two), two_from, extent)
        dst_total[...] += nt_dot(coef, query)
        coefs_ref[at - begin] = coef
        keep(new_coef, new_query, new_relation, third_query, third_relation)

    def step_with(work):
        def step(at, carry):
            one, two, two_start = after(at)
            if share <= NARROW:
                work(at, one, two, 0, two_start, share)
                return carry
            low, fits = window(at, start)
            two_low, two_fits = window(two, two_start)
            narrow = jnp.logical_and(fits, two_fits)

            @pl.when(narrow)
            def _():
                work(at, one, two, low, pl.multiple_of(two_start + two_low, 128), NARROW)

            @pl.when(jnp.logical_not(narrow))
            def _():
                work(at, one, two, 0, two_start, share)

            return carry

        return step

    light = begin
    if closing:
        light = jnp.minimum(end, begin + HELD)
        lax.fori_loop(begin, light, step_with(light_work), 0)
    lax.fori_loop(light, end, step_with(work), 0)
    src_grad_ref[...] = src_total[...].astype(src_grad_ref.dtype)
    if closing:
        dst_grad_ref[...] = dst_total[...].astype(dst_grad_ref.dtype)


def finish_kernel(packing, owners, place_ref, below_ref, keys_ref, src_grad_ref, rel_t_ref, dst_t_ref, coefs_ref, own_ref, src_total):
    share = own_ref.shape[0]
    at = pick(owners, place_ref[0])
    start = at * share
    begin = below_ref[at] // TILE
    end = jnp.maximum((below_ref[at + 1] + TILE - 1) // TILE, begin + 1)
    src_total[...] = src_grad_ref[...]

    def step(at, carry):
        word = keys_ref[pl.ds(at, 1), :]
        relation = nn_dot(rel_t_ref[...], one_hot(rel_t_ref.shape[1], packing.relation(word)))
        back = (nn_dot(dst_t_ref[...], coefs_ref[at - begin]) * relation).astype(jnp.bfloat16)
        source = one_hot(share, jnp.where(packing.is_empty(word), -1, packing.source(word) - start))
        src_total[...] += nt_dot(source, back)
        return carry

    lax.fori_loop(begin, jnp.minimum(end, begin + HELD), step, 0)
    own_ref[...] = src_total[...].astype(own_ref.dtype)


def update_kernel(place_ref, values_t_ref, scales_ref, accum_ref, arrived_ref, own_ref, returned_ref, piece_ref, low_ref, high_ref, state_ref, wide_scales):
    share = arrived_ref.shape[0]
    first = pl.multiple_of(place_ref[0] * share, 128)
    summed = arrived_ref[...].astype(jnp.float32) + own_ref[...].astype(jnp.float32)
    summed = (summed + returned_ref[...].astype(jnp.float32)).T
    wide_scales[...] = scales_ref[...].astype(jnp.float32)
    scale = scales_of(wide_scales, first, share)
    state = accum_ref[:, pl.ds(first, share)] + jnp.mean(summed * summed, axis=0, keepdims=True)
    updated = values_t_ref[...] - summed * (LEARN_RATE / (jnp.sqrt(state) + ROOT_EPSILON))
    piece = (updated * (1.0 / scale)).astype(piece_ref.dtype).T
    piece_ref[...] = piece
    low_ref[...] = piece[: share // 2]
    high_ref[...] = piece[share // 2 :]
    state_ref[...] = state


def place_kernel(tables, unit, place_ref, *refs):
    pieces, (out_ref, sems) = refs[: len(tables)], refs[-2:]
    place = place_ref[0]
    copies = []
    for k, (table, chosen) in enumerate(tables):
        row = pl.multiple_of(pick(table, place) * unit, 128)
        copies.append(pltpu.make_async_copy(pieces[k], out_ref.at[pl.ds(row, pieces[k].shape[0]), :], sems.at[k]))
    for act in ("start", "wait"):
        for copy, (_, chosen) in zip(copies, tables):
            if chosen is None:
                getattr(copy, act)()
            else:
                pl.when(pick(chosen, place) == 1)(getattr(copy, act))


SMEM = pl.BlockSpec(memory_space=pltpu.SMEM)
VMEM = pl.BlockSpec(memory_space=pltpu.VMEM)


ANY = pl.BlockSpec(memory_space=pl.ANY)
HBM = pl.BlockSpec(memory_space=pltpu.HBM)


def call(kernel, inputs, outs, scratch, name, us, scalars=1, unread=0, aliases={}, scalar_outs=(), in_hbm=0, out=None, grant=VMEM_LIMIT):
    return pl.pallas_call(
        kernel,
        out_shape=outs,
        in_specs=[SMEM] * scalars + [HBM] * in_hbm + [VMEM] * (len(inputs) - scalars - in_hbm - unread) + [ANY] * unread,
        out_specs=out or ([SMEM if at in scalar_outs else VMEM for at in range(len(outs))] if isinstance(outs, tuple) else VMEM),
        scratch_shapes=scratch,
        input_output_aliases=aliases,
        compiler_params=pltpu.CompilerParams(vmem_limit_bytes=grant),
        cost_estimate=pl.CostEstimate(flops=int(us * 1.15e9), bytes_accessed=0, transcendentals=0),
        name=name,
    )(*inputs)


def body(codes, scales, accum, relations, matching, edges, counts, negatives):
    reps = lax.axis_size("rep")
    at_rep = lax.axis_index("rep")
    place = at_rep[None]
    apart_dom = jnp.bitwise_xor(matching[0], lax.axis_index("dom"))
    part_rows, width = codes.shape
    slots = edges.shape[1]
    tiles = slots // GROUP
    negs = negatives.shape[1]
    share = part_rows // reps
    scales_row, accum_row = scales.reshape(part_rows // 128, 128), accum[None]
    wide_scales = pltpu.VMEM(scales_row.shape, jnp.float32)

    shape = jax.ShapeDtypeStruct
    ids_shape = shape((2 * tiles + 1, GROUP), jnp.int32)
    *sent, own_t, values_t, rel_t = call(
        functools.partial(open_kernel, tiles, share),
        (place, codes, scales_row, relations, edges, negatives, counts),
        (ids_shape,) * reps
        + (shape((width, share), jnp.bfloat16), shape((width, share), jnp.float32),
           shape(relations.shape[::-1], jnp.bfloat16)),
        [pltpu.VMEM((share, width), codes.dtype), pltpu.VMEM(scales_row.shape, scales.dtype),
         pltpu.VMEM(relations.shape, relations.dtype), pltpu.VMEM(edges.shape, edges.dtype),
         pltpu.VMEM(negatives.shape, negatives.dtype), pltpu.SMEM(counts.shape, counts.dtype),
         pltpu.VMEM((part_rows // LOW, tiles, LOW), jnp.float32), pltpu.SemaphoreType.DMA((6,)), wide_scales],
        "open", 3, in_hbm=6, grant=56 * 1024 * 1024)

    part = shape((share, width), jnp.bfloat16)
    part_sum = shape((share, width), jnp.float32)
    total = pltpu.VMEM((share, width), jnp.float32)
    packing = Packing(part_rows, share, relations.shape[0], reps * tiles)

    @jax.jit
    def sort_edges(place, *ids):
        return call(
            functools.partial(sort_kernel, packing, tiles, share), (place, *ids),
            (shape((reps * slots // TILE + 8, TILE), jnp.int32), shape((reps + 1,), jnp.int32),
             shape((8, 128), jnp.int32)),
            [pltpu.VMEM((8, 128), jnp.int32), pltpu.SemaphoreType.DMA], "sort", 5, scalar_outs=(1, 2))

    def gather_edges(place, codes, scales_row, *sent):
        ids = [sent[0]]
        for apart in range(1, reps):
            along = [(at, (at + apart) % reps) for at in range(reps)]
            ids.append(lax.ppermute(sent[apart], "rep", along))
        src_t = call(source_kernel, (codes, scales_row), shape((width, part_rows), jnp.bfloat16), [wide_scales], "source", 2, scalars=0)
        return (src_t, *ids) + tuple(sort_edges(place, *ids))

    dst_t, src_t, *ids, keys, below, ends = swap_beside(
        apart_dom, own_t, gather_edges, place, codes, scales_row, *sent)

    order = ring_order(reps)
    forward = [(order[i], order[(i + 1) % reps]) for i in range(reps)]

    def owners(behind):
        return [order[(order.index(z) - behind) % reps] for z in range(reps)]

    wide = shape((share, TILE), jnp.bfloat16)
    tall = shape((width, TILE), jnp.bfloat16)
    state = [wide, tall, tall, tall, tall]
    moving = arrived = None
    for behind in range(1, reps + 1):
        opening, closing = behind == 1, behind == reps
        table = owners(behind)
        chain = [owners(later) for later in range(behind, min(behind + 2, reps) + 1)]
        kept = shape((HELD, share, TILE), jnp.bfloat16)
        outs = (part_sum, part, kept) if closing else (part, part_sum, *state)
        scratch = ([pltpu.VMEM(kept.shape, kept.dtype) for kept in state] + [total] if closing else []) + [total]
        if opening:
            given = tuple(ids)
            outs += (part, shape((share, reps * tiles), jnp.bfloat16))
        else:
            given = (half, times, dst_grad) + held + (arrived if arrived is not None else below,)
        done = call(
            functools.partial(part_kernel, packing, chain, opening, closing, negs),
            (place, below, ends, keys, src_t, rel_t, dst_t) + given, outs, scratch, "part", 9,
            scalars=3, unread=0 if opening else 1,
            aliases={} if opening or closing else {9 + k: 1 + k for k in range(6)})
        src_grad, dst_grad = done[:2]
        held = tuple(done[2:7])
        if opening:
            half, times = done[7:]
            moving = src_grad
        elif not closing:
            arrived = lax.ppermute(moving, "rep", forward)
            moving = (arrived.astype(jnp.float32) + src_grad.astype(jnp.float32)).astype(jnp.bfloat16)
    arrived = lax.ppermute(moving, "rep", forward)
    @jax.jit
    def finish(*given):
        return call(functools.partial(finish_kernel, packing, table), given, part, [total], "finish", 3, scalars=2)

    returned, own = swap_beside(
        apart_dom, dst_grad, lambda *given: (finish(*given),), place, below, keys, src_grad, rel_t, dst_t, done[2])

    half_part = shape((share // 2, width), jnp.bfloat16)
    piece, low, high, state = call(
        update_kernel, (place, values_t, scales_row, accum_row, arrived, own, returned),
        (part, half_part, half_part, shape((1, share), jnp.float32)), [wide_scales], "update", 2)

    def put(tables, pieces, given, us):
        return call(
            functools.partial(place_kernel, tables, share // 2), (place, *pieces) + given, shape(codes.shape, jnp.bfloat16),
            [pltpu.SemaphoreType.DMA((len(pieces),))], "place", us, unread=len(given),
            aliases={1 + len(pieces): 0} if given else {}, out=HBM)

    if reps == 4:
        across = [(0, 2), (2, 0), (1, 3), (3, 1)]
        far = [lax.ppermute(held, "rep", across) for held in (low, high)]
        near = lax.ppermute(piece, "rep", [(0, 1), (1, 0), (2, 3), (3, 2)])
        middle = lax.ppermute(piece, "rep", [(1, 2), (2, 1)])
        ends = [lax.ppermute(held, "rep", [(2, 3), (1, 0)]) for held in far]
        early = [(piece, ([0, 2, 4, 6], None)), (near, ([2, 0, 6, 4], None))]
        early += [(held, ([4 + k, 6 + k, k, 2 + k], None)) for k, held in enumerate(far)]
        late = [(middle, ([6, 4, 2, 0], [0, 1, 1, 0]))]
        late += [(held, ([6 + k, 4 + k, 2 + k, k], [1, 0, 0, 1])) for k, held in enumerate(ends)]
    else:
        pieces = [piece]
        for behind in range(1, reps):
            pieces.append(lax.ppermute(pieces[-1], "rep", forward))
        early = [(held, ([2 * at for at in owners(behind)], None)) for behind, held in enumerate(pieces)]
        early, late = early[:-1], early[-1:]
    new_codes = put([table for _, table in early], [held for held, _ in early], (), 1)
    new_codes = put([table for _, table in late], [held for held, _ in late], (new_codes,), 1)
    return (new_codes, state[0])


def solution(mesh):
    placed = (
        P("dom", None),
        P("dom"),
        P("dom"),
        P(),
        P("dom"),
        P(None, ("dom", "rep")),
        P(("dom", "rep")),
        P(("dom", "rep"), None),
    )
    return jax.shard_map(
        body,
        mesh=mesh,
        in_specs=placed,
        out_specs=(P("dom", None), P(("dom", "rep"))),
        check_vma=False,
    )
```

```python
import functools

import jax
import jax.numpy as jnp
from jax import lax
from jax.experimental import pallas as pl
from jax.experimental.pallas import tpu as pltpu
from jax.sharding import PartitionSpec as P

GROUP = 512
LOW = 128
TILE = 512
NARROW = 256
HELD = 10
LAST_KEY = 2**31 - 1
LEARN_RATE = 0.1
ROOT_EPSILON = 1e-08
VMEM_LIMIT = 24 * 1024 * 1024


def swap_beside(apart, block, beside, *args):
    count = lax.axis_size("dom")

    def route(bits):
        return [(at, at ^ bits) for at in range(count)]

    if count <= 8:

        def branch(bits):
            return lambda block, *args: (lax.ppermute(block, "dom", route(bits)),) + beside(*args)

        return lax.switch(apart - 1, [branch(bits) for bits in range(1, count)], block, *args)
    for bit in range(count.bit_length() - 1):
        here = jnp.bitwise_and(jnp.right_shift(apart, bit), 1) == 1
        block = lax.cond(here, lambda b: lax.ppermute(b, "dom", route(1 << bit)), lambda b: b, block)
    return (block,) + beside(*args)


def ring_order(count):
    return list(range(0, count, 2)) + list(range(1, count, 2))[::-1]


def one_hot(rows, ids, one=1):
    step = min(rows, 256)
    spots = lax.broadcasted_iota(jnp.int32, (step, ids.shape[1]), 0).astype(jnp.bfloat16)
    low = (ids & (step - 1)).astype(jnp.float32)
    parts = []
    for first in range(0, rows, step):
        inside = (ids >= first) & (ids < first + step)
        key = jnp.where(inside, low, -1.0).astype(jnp.bfloat16)
        parts.append(jnp.where(spots == key, jnp.bfloat16(one), jnp.bfloat16(0)))
    return jnp.concatenate(parts, axis=0) if len(parts) > 1 else parts[0]


def nt_dot(a, b):
    return lax.dot_general(a, b, (((1,), (1,)), ((), ())), preferred_element_type=jnp.float32)


def nn_dot(a, b):
    return jnp.dot(a, b, preferred_element_type=jnp.float32)


def unpack(words):
    return jnp.concatenate([words & 0xFFFF, words >> 16], axis=0)


def bits_for(count):
    return (count - 1).bit_length()


class Packing:
    def __init__(self, part_rows, share, relations, blocks):
        self.half = part_rows // 2
        self.relation_at = bits_for(blocks)
        self.target_at = self.relation_at + bits_for(relations)
        self.source_at = self.target_at + bits_for(share + 1)
        assert self.source_at + bits_for(part_rows) <= 32

    def pack(self, source, target, relation, block):
        return (
            ((source - self.half) << self.source_at)
            + (target << self.target_at)
            + (relation << self.relation_at)
            + block
        )

    def bound(self, row):
        return (row - self.half) << self.source_at

    def source(self, word):
        return (word >> self.source_at) + self.half

    def target(self, word):
        return (word >> self.target_at) & ((1 << (self.source_at - self.target_at)) - 1)

    def relation(self, word):
        return (word >> self.relation_at) & ((1 << (self.target_at - self.relation_at)) - 1)

    def is_empty(self, word):
        return self.target(word) == (1 << (self.source_at - self.target_at)) - 1

    def block(self, word):
        return word & ((1 << self.relation_at) - 1)


def sort_columns(parts):
    count = len(parts)
    list_bits = bits_for(count)
    column = count * 8
    spread = max(1, TILE // column)
    low_lane_bits = bits_for(spread)
    lane_bits = [7 - low_lane_bits + k for k in range(low_lane_bits)] + list(range(7 - low_lane_bits))
    places = [("list", k) for k in range(list_bits)] + [("row", k) for k in range(3)] + [("lane", k) for k in lane_bits]
    row = lax.broadcasted_iota(jnp.int32, (8, 128), 0)
    lane = lax.broadcasted_iota(jnp.int32, (8, 128), 1)
    unset = {
        place: ((row if place[0] == "row" else lane) & (1 << place[1])) == 0
        for place in places
        if place[0] != "list"
    }
    total = len(places)

    def is_unset(index, position):
        if position == total:
            return True
        kind, bit = places[position]
        return index & (1 << bit) == 0 if kind == "list" else unset[(kind, bit)]

    def choose(mask, yes, no):
        if mask is True or mask is False:
            return yes if mask else no
        return jnp.where(mask, yes, no)

    for size in range(1, total + 1):
        for position in range(size - 1, -1, -1):
            kind, bit = places[position]
            if kind == "list":
                done = list(parts)
                for low in range(count):
                    high = low | 1 << bit
                    if high == low:
                        continue
                    up = is_unset(low, size)
                    small, large = jnp.minimum(parts[low], parts[high]), jnp.maximum(parts[low], parts[high])
                    done[low], done[high] = choose(up, small, large), choose(up, large, small)
                parts = done
                continue
            axis, extent = (0, 8) if kind == "row" else (1, 128)
            apart = 1 << bit
            first = unset[(kind, bit)]
            done = []
            for index, part in enumerate(parts):
                other = pltpu.roll(part, apart, axis)
                if 2 * apart != extent:
                    other = jnp.where(first, pltpu.roll(part, extent - apart, axis), other)
                small, large = jnp.minimum(part, other), jnp.maximum(part, other)
                up = is_unset(index, size)
                if up is True:
                    keep_small = first
                elif up is False:
                    keep_small = jnp.logical_not(first)
                else:
                    keep_small = jnp.logical_not(jnp.logical_xor(first, up))
                done.append(jnp.where(keep_small, small, large))
            parts = done
    return parts


def pick(table, place):
    out = jnp.int32(table[0])
    for at, entry in enumerate(table[1:], 1):
        out = jnp.where(place == at, jnp.int32(entry), out)
    return out


def open_kernel(tiles, share, place_ref, codes_hbm, scales_hbm, relations_hbm, edges_hbm, negatives_hbm, counts_hbm, *refs):
    refs, wide_scales = refs[:-1], refs[-1]
    reps = len(refs) - 11
    outs, refs = refs[:reps], refs[reps:]
    own_t_ref, values_t_ref, rel_t_ref, codes_ref, scales_ref, relations_ref, edges_ref, negatives_ref, counts_ref, counted, sems = refs
    place = place_ref[0]
    first = pl.multiple_of(place * share, 128)
    pairs = [
        (negatives_hbm, negatives_ref),
        (counts_hbm, counts_ref),
        (edges_hbm, edges_ref),
        (codes_hbm.at[pl.ds(first, share), :], codes_ref),
        (scales_hbm, scales_ref),
        (relations_hbm, relations_ref),
    ]
    copies = [pltpu.make_async_copy(source, target, sems.at[k]) for k, (source, target) in enumerate(pairs)]
    for copy in copies:
        copy.start()
    lanes = counted.shape[0]
    copies[0].wait()
    for block in range(tiles):
        negative = negatives_ref[block : block + 1, :]
        near = one_hot(LOW, negative & (LOW - 1))
        far = one_hot(lanes, negative >> (LOW.bit_length() - 1))
        held = nt_dot(far, near)
        for k in range(lanes):
            counted[k, block : block + 1, :] = held[k : k + 1, :]
    copies[1].wait()
    copies[2].wait()
    for apart, ids_ref in enumerate(outs):
        for tile in range(tiles):
            span = slice(tile * GROUP, (tile + 1) * GROUP)
            ids_ref[tile : tile + 1, :] = edges_ref[0:1, span] | (edges_ref[2:3, span] << 16)
        for tile in range(tiles // 2):
            near = edges_ref[1:2, tile * GROUP : (tile + 1) * GROUP]
            far = edges_ref[1:2, (tiles // 2 + tile) * GROUP : (tiles // 2 + tile + 1) * GROUP]
            ids_ref[tiles + tile : tiles + tile + 1, :] = near | (far << 16)
        to = place + apart
        to = jnp.where(to >= reps, to - reps, to)
        held = [counted[to * (share // LOW) + k] for k in range(share // LOW)]
        held += [jnp.zeros((tiles, GROUP - share), jnp.float32)] * (share < GROUP)
        held = jnp.concatenate(held, axis=1).astype(jnp.int32)
        ids_ref[3 * tiles // 2 : 2 * tiles, :] = held[: tiles // 2] | (held[tiles // 2 :] << 16)
        ids_ref[2 * tiles : 2 * tiles + 1, :] = jnp.full((1, GROUP), counts_ref[0], jnp.int32)
    for copy in copies[3:]:
        copy.wait()
    wide_scales[...] = scales_ref[...].astype(jnp.float32)
    values_t = codes_ref[...].T.astype(jnp.float32) * scales_of(wide_scales, first, share)
    values_t_ref[...] = values_t
    own_t_ref[...] = values_t.astype(jnp.bfloat16)
    rel_t_ref[...] = relations_ref[...].T


def scales_of(rows_ref, first, count):
    rows = [rows_ref[pl.ds(first // 128 + k, 1), :] for k in range(count // 128)]
    return jnp.concatenate(rows, axis=1)


def source_kernel(codes_ref, scales_ref, src_t_ref, wide_scales):
    codes_t = codes_ref[...].T.astype(jnp.float32)
    wide_scales[...] = scales_ref[...].astype(jnp.float32)
    src_t_ref[...] = (codes_t * scales_of(wide_scales, 0, codes_ref.shape[0])).astype(jnp.bfloat16)


def sort_kernel(packing, tiles, share, place_ref, *refs):
    ids_refs, (keys_ref, below_ref, ends_ref, ends_held, sem) = refs[:-5], refs[-5:]
    shards = len(ids_refs)
    first = place_ref[0] * share
    row = lax.broadcasted_iota(jnp.int32, (8, 128), 0)
    lane = lax.broadcasted_iota(jnp.int32, (8, 128), 1)
    keys, ranks, dead = [], [], jnp.zeros((1, 128), jnp.int32)
    for shard, ids_ref in enumerate(ids_refs):
        live = ids_ref[2 * tiles : 2 * tiles + 1, 0:128]
        relations = unpack(ids_ref[tiles : 3 * tiles // 2, :])
        for top in range(0, tiles, 8):
            for left in range(0, GROUP, 128):
                word = ids_ref[top : top + 8, left : left + 128]
                relation = relations[top : top + 8, left : left + 128]
                target = (word >> 16) - first
                target = jnp.where((target >= 0) & (target < share), target, share)
                key = packing.pack(word & 0xFFFF, target, relation, shard * tiles + top + row)
                over = (top + row) * GROUP + left + lane - live
                keys.append(jnp.where(over < 0, key, LAST_KEY))
                ranks.append(jnp.where(over < 0, LAST_KEY, over + dead))
        dead = dead + (tiles * GROUP - live)
    below = [jnp.int32(0)]
    for at in range(1, shards + 1):
        bound = LAST_KEY if at == shards else packing.bound(at * share)
        inside = functools.reduce(jnp.add, [jnp.where(key < bound, 1.0, 0.0) for key in keys])
        below.append(jnp.sum(inside).astype(jnp.int32))
    fill = [(below[at] - below[at + 1]) & (TILE - 1) for at in range(shards)]
    enough = functools.reduce(jnp.add, fill) <= len(keys) * 1024 - below[-1]
    filled = [jnp.int32(0)]
    for at in range(shards):
        filled.append(filled[at] + jnp.where(enough, fill[at], 0))
    for at in range(shards + 1):
        below_ref[at] = below[at] + filled[at]
    parts = []
    for key, rank in zip(keys, ranks):
        for at in range(shards - 2, -1, -1):
            key = jnp.where(rank < filled[at + 1], packing.bound((at + 1) * share) - 1, key)
        parts.append(key)
    parts = sort_columns(parts)
    ends_held[...] = jnp.zeros_like(ends_held)
    ends_held[0:1, :] = parts[0][0:1, :]
    ends_held[1:2, :] = parts[-1][7:8, :]
    copy = pltpu.make_async_copy(ends_held, ends_ref, sem)
    copy.start()
    columns = jnp.concatenate(parts, axis=0).T
    spread = max(1, TILE // columns.shape[1])
    rows = columns.shape[0] // spread
    for k in range(spread):
        keys_ref[:rows, k * columns.shape[1] : (k + 1) * columns.shape[1]] = columns[k * rows : (k + 1) * rows]
    keys_ref[rows:, :] = jnp.full((keys_ref.shape[0] - rows, TILE), LAST_KEY, jnp.int32)
    copy.wait()


def part_kernel(packing, tables, opening, closing, negs, place_ref, below_ref, ends_ref, keys_ref, src_t_ref, rel_t_ref, dst_t_ref, *refs):
    refs = list(refs)
    src_total = refs.pop()
    if closing:
        *refs, coef_ref, query_ref, relation_ref, new_query_ref, new_relation_ref, dst_total = refs
        half_ref, times_ref, before_ref, *given, after_ref, src_grad_ref, dst_grad_ref, coefs_ref = refs
        dst_total[...] = before_ref[...]
        for held, source in zip((coef_ref, query_ref, relation_ref, new_query_ref, new_relation_ref), given):
            held[...] = source[...]
    elif opening:
        *ids_refs, src_grad_ref, dst_total, coef_ref, query_ref, relation_ref, new_query_ref, new_relation_ref, half_ref, times_ref = refs
        half_ref[...] = dst_t_ref[...].T * jnp.bfloat16(0.5)
        tiles = ids_refs[0].shape[0] // 2
        counted = [unpack(ids_ref[3 * tiles // 2 : 2 * tiles, : half_ref.shape[0]]) for ids_ref in ids_refs]
        counted = jnp.concatenate(counted, axis=0).astype(jnp.float32) * (0.5 / negs)
        times_ref[...] = counted.T.astype(times_ref.dtype)
        dst_total[...] = jnp.zeros_like(dst_total)
    else:
        half_ref, times_ref = refs[:2]
        src_grad_ref, dst_total, coef_ref, query_ref, relation_ref, new_query_ref, new_relation_ref = refs[-7:]
    share, width = half_ref.shape

    def span(table):
        at = pick(table, place_ref[0])
        start = pl.multiple_of(at * share, 128)
        begin = below_ref[at] // TILE
        return start, begin, jnp.maximum((below_ref[at + 1] + TILE - 1) // TILE, begin + 1)

    spans = [span(table) for table in tables]
    spans = spans + spans[-1:] * (3 - len(spans))
    start, begin, end = spans[0]
    src_total[...] = jnp.zeros_like(src_total)
    last_row = keys_ref.shape[0] - 9

    def after(at):
        (_, _, end0), (start1, begin1, end1), (start2, begin2, _) = spans
        over, soon, over1 = at + 1 >= end0, at + 2 >= end0, begin1 + 1 >= end1
        one = jnp.where(over, begin1, at + 1)
        two = jnp.where(over, jnp.where(over1, begin2, begin1 + 1), jnp.where(soon, begin1, at + 2))
        two_start = jnp.where(over, jnp.where(over1, start2, start1), jnp.where(soon, start1, start))
        return one, two, pl.multiple_of(two_start, 128)

    def word_of(at):
        return keys_ref[pl.ds(at, 1), :]

    def window(at, start):
        at = jnp.minimum(at, last_row)
        low = packing.source(ends_ref[0, at]) - start
        high = packing.source(ends_ref[1, at + 127 - last_row]) - start
        low = jnp.clip((low >> 7) << 7, 0, share - NARROW)
        return pl.multiple_of(low, 128), jnp.minimum(high, share - 1) - low < NARROW

    def sources(word, start, extent):
        return one_hot(extent, jnp.where(packing.is_empty(word), -1, packing.source(word) - start))

    def query_of(word, start, extent):
        relation = nn_dot(rel_t_ref[...], one_hot(rel_t_ref.shape[1], packing.relation(word)))
        relation = relation.astype(jnp.bfloat16)
        found = nn_dot(src_t_ref[:, pl.ds(start, extent)], sources(word, start, extent))
        return found.astype(jnp.bfloat16) * relation, relation

    def coef_of(word, query):
        times = nn_dot(times_ref[...], one_hot(times_ref.shape[1], packing.block(word))).astype(jnp.bfloat16)
        bend = jnp.tanh(nn_dot(half_ref[...], query))
        below = (bend - 1.0).astype(jnp.bfloat16)
        return times * (bend + 1.0).astype(jnp.bfloat16) + one_hot(share, packing.target(word), 0.5) * below

    def keep(coef, query, relation, new_query, new_relation):
        coef_ref[...] = coef
        query_ref[...] = query
        relation_ref[...] = relation
        new_query_ref[...] = new_query
        new_relation_ref[...] = new_relation

    if opening:
        query, relation = query_of(word_of(begin), start, share)
        one, _, _ = after(begin)
        one_start = pl.multiple_of(jnp.where(begin + 1 >= end, spans[1][0], start), 128)
        new_query, new_relation = query_of(word_of(one), one_start, share)
        keep(coef_of(word_of(begin), query), query, relation, new_query, new_relation)

    def work(at, one, two, low, two_from, extent):
        coef, query, relation = coef_ref[...], query_ref[...], relation_ref[...]
        new_query, new_relation = new_query_ref[...], new_relation_ref[...]
        back = nn_dot(dst_t_ref[...], coef)
        third_query, third_relation = query_of(word_of(two), two_from, extent)
        new_coef = coef_of(word_of(one), new_query)
        dst_total[...] += nt_dot(coef, query)
        back = back.astype(jnp.bfloat16) * relation
        src_total[pl.ds(low, extent), :] += nt_dot(sources(word_of(at), start + low, extent), back)
        keep(new_coef, new_query, new_relation, third_query, third_relation)

    def light_work(at, one, two, low, two_from, extent):
        coef, query = coef_ref[...], query_ref[...]
        new_query, new_relation = new_query_ref[...], new_relation_ref[...]
        third_query, third_relation = query_of(word_of(two), two_from, extent)
        new_coef = coef_of(word_of(one), new_query)
        dst_total[...] += nt_dot(coef, query)
        coefs_ref[at - begin] = coef
        keep(new_coef, new_query, new_relation, third_query, third_relation)

    def step_with(work):
        def step(at, carry):
            one, two, two_start = after(at)
            if share <= NARROW:
                work(at, one, two, 0, two_start, share)
                return carry
            low, fits = window(at, start)
            two_low, two_fits = window(two, two_start)
            narrow = jnp.logical_and(fits, two_fits)

            @pl.when(narrow)
            def _():
                work(at, one, two, low, pl.multiple_of(two_start + two_low, 128), NARROW)

            @pl.when(jnp.logical_not(narrow))
            def _():
                work(at, one, two, 0, two_start, share)

            return carry

        return step

    light = begin
    if closing:
        light = jnp.minimum(end, begin + HELD)
        lax.fori_loop(begin, light, step_with(light_work), 0)
    lax.fori_loop(light, end, step_with(work), 0)
    src_grad_ref[...] = src_total[...].astype(src_grad_ref.dtype)
    if closing:
        dst_grad_ref[...] = dst_total[...].astype(dst_grad_ref.dtype)


def finish_kernel(packing, owners, place_ref, below_ref, keys_ref, src_grad_ref, rel_t_ref, dst_t_ref, coefs_ref, own_ref, src_total):
    share = own_ref.shape[0]
    at = pick(owners, place_ref[0])
    start = at * share
    begin = below_ref[at] // TILE
    end = jnp.maximum((below_ref[at + 1] + TILE - 1) // TILE, begin + 1)
    src_total[...] = src_grad_ref[...]

    def step(at, carry):
        word = keys_ref[pl.ds(at, 1), :]
        relation = nn_dot(rel_t_ref[...], one_hot(rel_t_ref.shape[1], packing.relation(word)))
        back = (nn_dot(dst_t_ref[...], coefs_ref[at - begin]) * relation).astype(jnp.bfloat16)
        source = one_hot(share, jnp.where(packing.is_empty(word), -1, packing.source(word) - start))
        src_total[...] += nt_dot(source, back)
        return carry

    lax.fori_loop(begin, jnp.minimum(end, begin + HELD), step, 0)
    own_ref[...] = src_total[...].astype(own_ref.dtype)


def hold_kernel(piece_ref, after_ref, held_ref):
    held_ref[...] = piece_ref[...]


def update_kernel(place_ref, values_t_ref, scales_ref, accum_ref, arrived_ref, own_ref, returned_ref, piece_ref, low_ref, high_ref, state_ref, wide_scales):
    share = arrived_ref.shape[0]
    first = pl.multiple_of(place_ref[0] * share, 128)
    summed = arrived_ref[...].astype(jnp.float32) + own_ref[...].astype(jnp.float32)
    summed = (summed + returned_ref[...].astype(jnp.float32)).T
    wide_scales[...] = scales_ref[...].astype(jnp.float32)
    scale = scales_of(wide_scales, first, share)
    state = accum_ref[:, pl.ds(first, share)] + jnp.mean(summed * summed, axis=0, keepdims=True)
    updated = values_t_ref[...] - summed * (LEARN_RATE / (jnp.sqrt(state) + ROOT_EPSILON))
    piece = (updated * (1.0 / scale)).astype(piece_ref.dtype).T
    piece_ref[...] = piece
    low_ref[...] = piece[: share // 2]
    high_ref[...] = piece[share // 2 :]
    state_ref[...] = state


def place_kernel(tables, unit, place_ref, *refs):
    pieces, (out_ref, sems) = refs[: len(tables)], refs[-2:]
    place = place_ref[0]
    copies = []
    for k, (table, chosen) in enumerate(tables):
        row = pl.multiple_of(pick(table, place) * unit, 128)
        copies.append(pltpu.make_async_copy(pieces[k], out_ref.at[pl.ds(row, pieces[k].shape[0]), :], sems.at[k]))
    for act in ("start", "wait"):
        for copy, (_, chosen) in zip(copies, tables):
            if chosen is None:
                getattr(copy, act)()
            else:
                pl.when(pick(chosen, place) == 1)(getattr(copy, act))


SMEM = pl.BlockSpec(memory_space=pltpu.SMEM)
VMEM = pl.BlockSpec(memory_space=pltpu.VMEM)


ANY = pl.BlockSpec(memory_space=pl.ANY)
HBM = pl.BlockSpec(memory_space=pltpu.HBM)


def call(kernel, inputs, outs, scratch, name, us, scalars=1, unread=0, aliases={}, scalar_outs=(), in_hbm=0, out=None, grant=VMEM_LIMIT):
    return pl.pallas_call(
        kernel,
        out_shape=outs,
        in_specs=[SMEM] * scalars + [HBM] * in_hbm + [VMEM] * (len(inputs) - scalars - in_hbm - unread) + [ANY] * unread,
        out_specs=out or ([SMEM if at in scalar_outs else VMEM for at in range(len(outs))] if isinstance(outs, tuple) else VMEM),
        scratch_shapes=scratch,
        input_output_aliases=aliases,
        compiler_params=pltpu.CompilerParams(vmem_limit_bytes=grant),
        cost_estimate=pl.CostEstimate(flops=int(us * 1.15e9), bytes_accessed=0, transcendentals=0),
        name=name,
    )(*inputs)


def body(codes, scales, accum, relations, matching, edges, counts, negatives):
    reps = lax.axis_size("rep")
    at_rep = lax.axis_index("rep")
    place = at_rep[None]
    apart_dom = jnp.bitwise_xor(matching[0], lax.axis_index("dom"))
    part_rows, width = codes.shape
    slots = edges.shape[1]
    tiles = slots // GROUP
    negs = negatives.shape[1]
    share = part_rows // reps
    scales_row, accum_row = scales.reshape(part_rows // 128, 128), accum[None]
    wide_scales = pltpu.VMEM(scales_row.shape, jnp.float32)

    shape = jax.ShapeDtypeStruct
    ids_shape = shape((2 * tiles + 1, GROUP), jnp.int32)
    *sent, own_t, values_t, rel_t = call(
        functools.partial(open_kernel, tiles, share),
        (place, codes, scales_row, relations, edges, negatives, counts),
        (ids_shape,) * reps
        + (shape((width, share), jnp.bfloat16), shape((width, share), jnp.float32),
           shape(relations.shape[::-1], jnp.bfloat16)),
        [pltpu.VMEM((share, width), codes.dtype), pltpu.VMEM(scales_row.shape, scales.dtype),
         pltpu.VMEM(relations.shape, relations.dtype), pltpu.VMEM(edges.shape, edges.dtype),
         pltpu.VMEM(negatives.shape, negatives.dtype), pltpu.SMEM(counts.shape, counts.dtype),
         pltpu.VMEM((part_rows // LOW, tiles, LOW), jnp.float32), pltpu.SemaphoreType.DMA((6,)), wide_scales],
        "open", 3, in_hbm=6, grant=56 * 1024 * 1024)

    part = shape((share, width), jnp.bfloat16)
    part_sum = shape((share, width), jnp.float32)
    total = pltpu.VMEM((share, width), jnp.float32)
    packing = Packing(part_rows, share, relations.shape[0], reps * tiles)

    @jax.jit
    def sort_edges(place, *ids):
        return call(
            functools.partial(sort_kernel, packing, tiles, share), (place, *ids),
            (shape((reps * slots // TILE + 8, TILE), jnp.int32), shape((reps + 1,), jnp.int32),
             shape((8, 128), jnp.int32)),
            [pltpu.VMEM((8, 128), jnp.int32), pltpu.SemaphoreType.DMA], "sort", 5, scalar_outs=(1, 2))

    def gather_edges(place, codes, scales_row, *sent):
        ids = [sent[0]]
        for apart in range(1, reps):
            along = [(at, (at + apart) % reps) for at in range(reps)]
            ids.append(lax.ppermute(sent[apart], "rep", along))
        src_t = call(source_kernel, (codes, scales_row), shape((width, part_rows), jnp.bfloat16), [wide_scales], "source", 2, scalars=0)
        return (src_t, *ids) + tuple(sort_edges(place, *ids))

    dst_t, src_t, *ids, keys, below, ends = swap_beside(
        apart_dom, own_t, gather_edges, place, codes, scales_row, *sent)

    order = ring_order(reps)
    forward = [(order[i], order[(i + 1) % reps]) for i in range(reps)]

    def owners(behind):
        return [order[(order.index(z) - behind) % reps] for z in range(reps)]

    wide = shape((share, TILE), jnp.bfloat16)
    tall = shape((width, TILE), jnp.bfloat16)
    state = [wide, tall, tall, tall, tall]
    moving = arrived = None
    for behind in range(1, reps + 1):
        opening, closing = behind == 1, behind == reps
        table = owners(behind)
        chain = [owners(later) for later in range(behind, min(behind + 2, reps) + 1)]
        kept = shape((HELD, share, TILE), jnp.bfloat16)
        outs = (part_sum, part, kept) if closing else (part, part_sum, *state)
        scratch = ([pltpu.VMEM(kept.shape, kept.dtype) for kept in state] + [total] if closing else []) + [total]
        if opening:
            given = tuple(ids)
            outs += (part, shape((share, reps * tiles), jnp.bfloat16))
        else:
            given = (half, times, dst_grad) + held + (arrived if arrived is not None else below,)
        done = call(
            functools.partial(part_kernel, packing, chain, opening, closing, negs),
            (place, below, ends, keys, src_t, rel_t, dst_t) + given, outs, scratch, "part", 9,
            scalars=3, unread=0 if opening else 1,
            aliases={} if opening or closing else {9 + k: 1 + k for k in range(6)})
        src_grad, dst_grad = done[:2]
        held = tuple(done[2:7])
        if opening:
            half, times = done[7:]
            moving = src_grad
        elif not closing:
            arrived = lax.ppermute(moving, "rep", forward)
            moving = (arrived.astype(jnp.float32) + src_grad.astype(jnp.float32)).astype(jnp.bfloat16)
    arrived = lax.ppermute(moving, "rep", forward)
    @jax.jit
    def finish(*given):
        return call(functools.partial(finish_kernel, packing, table), given, part, [total], "finish", 3, scalars=2)

    returned, own = swap_beside(
        apart_dom, dst_grad, lambda *given: (finish(*given),), place, below, keys, src_grad, rel_t, dst_t, done[2])

    half_part = shape((share // 2, width), jnp.bfloat16)
    piece, low, high, state = call(
        update_kernel, (place, values_t, scales_row, accum_row, arrived, own, returned),
        (part, half_part, half_part, shape((1, share), jnp.float32)), [wide_scales], "update", 2)

    def put(tables, pieces, given, us):
        return call(
            functools.partial(place_kernel, tables, share // 2), (place, *pieces) + given, shape(codes.shape, jnp.bfloat16),
            [pltpu.SemaphoreType.DMA((len(pieces),))], "place", us, unread=len(given),
            aliases={1 + len(pieces): 0} if given else {}, out=HBM)

    if reps == 4:
        across = [(0, 2), (2, 0), (1, 3), (3, 1)]
        far = [lax.ppermute(held, "rep", across) for held in (low, high)]
        near = lax.ppermute(piece, "rep", [(0, 1), (1, 0), (2, 3), (3, 2)])
        held = call(hold_kernel, (piece, far[0]), part, [], "hold", 1, scalars=0, unread=1)
        middle = lax.ppermute(held, "rep", [(1, 2), (2, 1)])
        ends = [lax.ppermute(held, "rep", [(2, 3), (1, 0)]) for held in far]
        early = [(piece, ([0, 2, 4, 6], None)), (near, ([2, 0, 6, 4], None))]
        early += [(held, ([4 + k, 6 + k, k, 2 + k], None)) for k, held in enumerate(far)]
        late = [(middle, ([6, 4, 2, 0], [0, 1, 1, 0]))]
        late += [(held, ([6 + k, 4 + k, 2 + k, k], [1, 0, 0, 1])) for k, held in enumerate(ends)]
    else:
        pieces = [piece]
        for behind in range(1, reps):
            pieces.append(lax.ppermute(pieces[-1], "rep", forward))
        early = [(held, ([2 * at for at in owners(behind)], None)) for behind, held in enumerate(pieces)]
        early, late = early[:-1], early[-1:]
    new_codes = put([table for _, table in early], [held for held, _ in early], (), 1)
    new_codes = put([table for _, table in late], [held for held, _ in late], (new_codes,), 1)
    return (new_codes, state[0])


def solution(mesh):
    placed = (
        P("dom", None),
        P("dom"),
        P("dom"),
        P(),
        P("dom"),
        P(None, ("dom", "rep")),
        P(("dom", "rep")),
        P(("dom", "rep"), None),
    )
    return jax.shard_map(
        body,
        mesh=mesh,
        in_specs=placed,
        out_specs=(P("dom", None), P(("dom", "rep"))),
        check_vma=False,
    )
```
